32 devices in a mesh: leaf: 32 (over z, y, x, core).
Axes of the slice: x: 2, y: 2, z: 4, core: 2. Of those that a mesh axis runs over, the one named last changes fastest.
Arguments:
- nodes: float32 [4, 131072], P(None, 'leaf'), as said below
- inputs: bfloat16 [64, 131072], P(None, 'leaf'), may hold values from -6 to 6
- leaf_basis: bfloat16 [64, 131072], P(None, 'leaf'), may hold values from -0.375 to 0.375
- leaf_transfer: bfloat16 [512, 64, 64], P('leaf'), may hold values from -0.1875 to 0.1875
- upper_transfer: bfloat16 [3, 32, 2, 64, 64], P(None, 'leaf'), as said below
- coupling: bfloat16 [4, 32, 3, 64, 64], P(None, 'leaf'), as said below
- near_cols: int32 [512, 12], P('leaf'), may hold values from 0 to 511, as said below
- near_count: int32 [512], P('leaf'), may hold values from 1 to 12, as said below
Outputs:
- result: bfloat16 [64, 131072], P(None, 'leaf')
The draws below stay inside these ranges and needn't reach their ends.
Inputs may be any that keep to these rules, and one draw needn't show every extreme that they name: `near_cols`: slot 0 of leaf cluster t is t itself; every entry lies within 8 of t, and an entry exactly 8 away occurs. `near_count`: on one or more devices every leaf cluster has 12 live slots. upper_transfer[b, d] is the same for all devices d with equal d // 2^(b+1). coupling[b, d] is the same for all devices d with equal d // 2^b. `nodes`: row 3 is positive.
All inputs are finite; a program needn't handle non-finite values.
Results may differ from the reference program's by a relative error of at most 0.0049.
Values may be sent and summed in bfloat16 or wider, within the bound.
No kernel may reach another device: no remote copies, remote signals or barrier semaphores. Data moves between devices by JAX's collectives and lax.ppermute only.
A program may use at most 64 MiB of HBM per device.

```python
import math
import jax
import jax.numpy as jnp
from jax import lax

B = 256
K = 64
R = 64
LEAF_DEV = 16
NEAR = 12
HALO = 8
UPPER = 3
LEVC = 4
NLEAF = 512
NPTS = 131072
N_LEAF = 32


def draw_nodes(key, part):
    place_key, weight_key = jax.random.split(key)
    fraction = jax.random.uniform(place_key, (3, NLEAF, B), jnp.float32)
    weights = jnp.exp(jax.random.uniform(weight_key, (1, NLEAF, B), jnp.float32, math.log(0.01), math.log(0.1)))
    leaf_start = (jnp.arange(NLEAF).astype(jnp.float32) / (8 * HALO))[None, :, None]
    offset_rows = jnp.concatenate([leaf_start, jnp.zeros((2, NLEAF, 1), jnp.float32)], axis=0)
    coords = fraction + offset_rows
    return jnp.concatenate([coords, weights], axis=0).reshape(4, NLEAF * B)


def replicate_levels(raw_values, extra_bits, scales):
    device_ids = jnp.arange(N_LEAF)
    stacked = []
    for height in range(raw_values.shape[0]):
        owner = device_ids >> height + extra_bits << height + extra_bits
        stacked.append(raw_values[height][owner] * scales[height])
    return jnp.stack(stacked)


def draw_upper_transfer(key, part):
    shape_full = (UPPER, N_LEAF, 2, K, K)
    raw_values = jax.random.normal(key, shape_full, jnp.float32)
    scales = [1.0 / math.sqrt(2.0 * K) for height in range(UPPER)]
    return replicate_levels(raw_values, 1, scales).astype(jnp.bfloat16)


def draw_coupling(key, part):
    shape_full = (LEVC, N_LEAF, 3, K, K)
    raw_values = jax.random.normal(key, shape_full, jnp.float32)
    scales = [math.sqrt(2.0) ** height / math.sqrt(3.0 * K) for height in range(LEVC)]
    return replicate_levels(raw_values, 0, scales).astype(jnp.bfloat16)


def draw_near_cols(key, part):
    order_key, sign_key = jax.random.split(key)
    span_count = 2 * HALO
    scores = jax.random.randint(order_key, (NLEAF, span_count), 0, 1 << 20) * span_count + jnp.arange(span_count)[None, :]
    ranking = jnp.argsort(scores, axis=1)
    table = jnp.concatenate([jnp.arange(-HALO, 0), jnp.arange(1, HALO + 1)])
    offsets = table[ranking][:, :NEAR - 1]
    signs = jax.random.randint(sign_key, (NLEAF, 1), 0, 2) * 2 - 1
    offsets = jnp.concatenate([signs * HALO, offsets[:, 1:]], axis=1)
    row_ids = jnp.arange(NLEAF)[:, None]
    target = row_ids + offsets
    inside = (target >= 0) & (target < NLEAF)
    target = jnp.where(inside, target, row_ids - offsets)
    return jnp.concatenate([row_ids, target], axis=1).astype(jnp.int32)


def draw_near_count(key, part):
    cap_key, busy_key, count_key = jax.random.split(key, 3)
    devices = NLEAF // LEAF_DEV
    caps = jax.random.randint(cap_key, (devices,), NEAR // 4 + 1, NEAR // 2 + 2)
    first_busy = jax.random.randint(busy_key, (), 0, devices)
    busy = (jnp.arange(devices) - first_busy) % devices < max(1, devices // 16)
    caps = jnp.where(busy, NEAR, caps)
    leaf_caps = jnp.repeat(caps, LEAF_DEV)
    counts = jax.random.randint(count_key, (NLEAF,), 0, 1 << 20) % leaf_caps + 1
    counts = jnp.where(jnp.repeat(busy, LEAF_DEV), NEAR, counts)
    return counts.astype(jnp.int32)


def levels(rng, shape, shards, low, high):
    factor_of = 1.0
    for dim, blocks in shards:
        heights = jax.random.uniform(jax.random.fold_in(jax.random.fold_in(rng, 6), dim), (blocks,), jnp.float32, low / len(shards), high / len(shards))
        factor_of = factor_of * jnp.repeat(jnp.exp(heights), shape[dim] // blocks).reshape((-1,) + (1,) * (len(shape) - 1 - dim))
    return factor_of


def noise(rng, shape, scale, limit, cuts=(), kind=jnp.bfloat16):
    gain = levels(rng, shape, cuts, -0.22, 0.18) if cuts else 1.0
    entries = jax.random.normal(rng, shape, jnp.float32) * scale * gain
    return jnp.minimum(jnp.maximum(entries, -limit), limit).astype(kind)


def setup_inputs(seed: int = 0) -> dict:
    key_of = jax.random.split(jax.random.key(seed), 9)
    nodes = draw_nodes(jax.random.fold_in(key_of[8], 71), 0)
    inputs = noise(key_of[1], (R, NPTS), 1.0, 6.0, ((1, 32),))
    leaf_basis = noise(key_of[2], (K, NPTS), B ** -0.5, 0.375, ((1, 32),))
    leaf_transfer = noise(key_of[3], (NLEAF, K, K), (K * LEAF_DEV) ** -0.5, 0.1875, ((0, 32),))
    upper_transfer = draw_upper_transfer(jax.random.fold_in(key_of[8], 71), 0)
    coupling = draw_coupling(jax.random.fold_in(key_of[8], 71), 0)
    near_cols = draw_near_cols(jax.random.fold_in(key_of[8], 71), 0)
    near_count = draw_near_count(jax.random.fold_in(key_of[8], 71), 0)
    return {"nodes": nodes, "inputs": inputs, "leaf_basis": leaf_basis, "leaf_transfer": leaf_transfer, "upper_transfer": upper_transfer, "coupling": coupling, "near_cols": near_cols, "near_count": near_count}


wave_number = 2.0
core_width = 0.05
highest = lax.Precision.HIGHEST

def kernel_tile(row_nodes, col_nodes):
    squared = jnp.zeros((row_nodes.shape[1], row_nodes.shape[2], col_nodes.shape[2]), jnp.float32)
    for component in range(3):
        spread = row_nodes[component][:, :, None] - col_nodes[component][:, None, :]
        squared = squared + spread * spread
    radius = jnp.sqrt(squared)
    return col_nodes[3][:, None, :] * jnp.cos(wave_number * radius) * lax.rsqrt(squared + core_width * core_width)

def rounded(values):
    return lax.optimization_barrier(values.astype(jnp.bfloat16)).astype(jnp.float32)

def near_field(nodes, inputs, near_cols, near_count):
    all_nodes = nodes.reshape(4, NLEAF, B)
    all_inputs = inputs.reshape(R, NLEAF, B)
    own_groups = jnp.moveaxis(all_nodes.reshape(4, N_LEAF, LEAF_DEV, B), 1, 0)
    col_groups = near_cols.reshape(N_LEAF, LEAF_DEV, NEAR)
    count_groups = near_count.reshape(N_LEAF, LEAF_DEV)

    def one_group(group):
        own_nodes, columns_all, counts = group

        def one_slot(slot_index, running):
            column = lax.dynamic_index_in_dim(columns_all, slot_index, 1, keepdims=False)
            col_nodes = jnp.take(all_nodes, column, axis=1)
            col_inputs = jnp.take(all_inputs, column, axis=1)
            near_tile = kernel_tile(own_nodes, col_nodes).astype(jnp.bfloat16)
            contrib = jnp.einsum('lib,rlb->rli', near_tile.astype(jnp.float32), col_inputs.astype(jnp.float32), precision=highest)
            live_mask = (slot_index < counts).astype(jnp.float32)
            return running + contrib * live_mask[None, :, None]
        start_value = jnp.zeros((R, LEAF_DEV, B), jnp.float32)
        return lax.fori_loop(0, NEAR, one_slot, start_value)
    blocks = lax.map(one_group, (own_groups, col_groups, count_groups))
    return jnp.moveaxis(blocks, 0, 1).reshape(R, NLEAF * B)

def far_field(inputs, leaf_basis, leaf_transfer, upper_transfer, coupling):
    leaf_bases = leaf_basis.reshape(K, NLEAF, B).astype(jnp.float32)
    leaf_moments = jnp.einsum('klb,rlb->lkr', leaf_bases, inputs.reshape(R, NLEAF, B).astype(jnp.float32), precision=highest).astype(jnp.bfloat16)
    transfers = leaf_transfer.reshape(N_LEAF, LEAF_DEV, K, K).astype(jnp.float32)
    moment = jnp.einsum('dlkj,dlkr->djr', transfers, leaf_moments.reshape(N_LEAF, LEAF_DEV, K, R).astype(jnp.float32), precision=highest).astype(jnp.bfloat16)
    moments = [moment]
    for height in range(UPPER):
        pairs = upper_transfer[height, ::2 << height].astype(jnp.float32)
        children = moments[-1].astype(jnp.float32).reshape(-1, 2, K, R)
        lifted = jnp.einsum('ckj,ckr->cjr', pairs[:, 0], children[:, 0], precision=highest) + jnp.einsum('ckj,ckr->cjr', pairs[:, 1], children[:, 1], precision=highest)
        moments.append(lifted.astype(jnp.bfloat16))
    far_terms = []
    for height in range(LEVC):
        current = moments[height].astype(jnp.float32)
        clusters = current.shape[0]
        padded = jnp.pad(current, ((3, 3), (0, 0), (0, 0)))

        def taken(offset):
            return padded[3 + offset:3 + offset + clusters]
        is_even = (jnp.arange(clusters) % 2 == 0)[:, None, None]
        slot_one = jnp.where(is_even, taken(-2), taken(-3))
        slot_two = jnp.where(is_even, taken(2), taken(-2))
        slot_three = jnp.where(is_even, taken(3), taken(2))
        matrices = coupling[height, ::1 << height].astype(jnp.float32)
        term = jnp.einsum('ckj,cjr->ckr', matrices[:, 0], slot_one, precision=highest)
        term = term + jnp.einsum('ckj,cjr->ckr', matrices[:, 1], slot_two, precision=highest)
        term = term + jnp.einsum('ckj,cjr->ckr', matrices[:, 2], slot_three, precision=highest)
        far_terms.append(term)
    coeffs = far_terms[LEVC - 1]
    for height in range(UPPER - 1, -1, -1):
        pairs = upper_transfer[height, ::2 << height].astype(jnp.float32)
        child_part = jnp.einsum('cskj,cjr->cskr', pairs, rounded(coeffs), precision=highest).reshape(-1, K, R)
        coeffs = far_terms[height] + child_part
    leaf_coef = jnp.einsum('dlkj,djr->dlkr', transfers, rounded(coeffs), precision=highest).astype(jnp.bfloat16).reshape(NLEAF, K, R)
    far_part = jnp.einsum('lkr,klb->rlb', leaf_coef.astype(jnp.float32), leaf_bases, precision=highest)
    return far_part.reshape(R, NLEAF * B)

def reference(nodes, inputs, leaf_basis, leaf_transfer, upper_transfer, coupling, near_cols, near_count):
    near_part = near_field(nodes, inputs, near_cols, near_count)
    far_part = far_field(inputs, leaf_basis, leaf_transfer, upper_transfer, coupling)
    return (near_part + far_part).astype(jnp.bfloat16)
```

```python
import functools

import jax
import jax.numpy as jnp
from jax import lax
from jax.experimental import pallas as pl
from jax.experimental.pallas import tpu as pltpu
from jax.sharding import PartitionSpec as P

f32 = jnp.float32
bf16 = jnp.bfloat16
HALO = 8
WAVE = 2.0
CORE2 = 0.05 * 0.05

RANGE2 = 4.5
LAM = 0.07457663918345607
MU = -1.1742618906652897
A2, A1, A0 = 2.3170164265523123, 2.436862577578775, -0.8205262732930618
SQLAM = LAM**0.5
BFMAX = 3.3895e38
KF = 48
UNROLL = 4
LIST = 256
NT = (((1,), (1,)), ((), ()))
TN = (((0,), (0,)), ((), ()))

VM = pl.BlockSpec(memory_space=pltpu.VMEM)
SM = pl.BlockSpec(memory_space=pltpu.SMEM)
HBM = pl.BlockSpec(memory_space=pltpu.HBM)


def call(body, name, outs, specs_in, specs_out, scratch=(), aliases=None, us=1.0, vmem=16):
    return pl.pallas_call(
        body,
        name=name,
        out_shape=outs,
        in_specs=specs_in,
        out_specs=specs_out,
        scratch_shapes=list(scratch),
        input_output_aliases=aliases or {},
        compiler_params=pltpu.CompilerParams(vmem_limit_bytes=vmem << 20),
        cost_estimate=pl.CostEstimate(
            flops=int(us * 1e9), bytes_accessed=int(us * 1e6), transcendentals=0
        ),
    )


def pieces(x):
    hi = jnp.clip(x, -BFMAX, BFMAX).astype(bf16).astype(f32)
    mid = (x - hi).astype(bf16).astype(f32)
    low = (x - hi - mid).astype(bf16).astype(f32)
    return hi, mid, low


def row_features(x, y, z):
    n = LAM * (x * x + y * y + z * z)
    one = jnp.ones_like(x)
    zero = jnp.zeros_like(x)
    hi, mid, low = pieces(jnp.concatenate([x, y, z, n, one, zero, zero, zero], axis=0))
    return jnp.concatenate([hi, mid, hi, low, hi, mid], axis=0)


def column_features(x, y, z):
    n = LAM * (x * x + y * y + z * z + CORE2)
    one = jnp.ones_like(x)
    zero = jnp.zeros_like(x)
    k = -2.0 * LAM
    hi, mid, low = pieces(
        jnp.concatenate([k * x, k * y, k * z, one, n, zero, zero, zero], axis=0)
    )
    return jnp.concatenate([hi, hi, mid, hi, low, mid], axis=0)


def prepare(
    dev, nodes_hbm, inputs_hbm, basis_hbm, transfer_hbm,
    to_chip, to_next, v_own, rows, cols, own_xyz, box, moment,
    nodes, inputs, basis, transfer, sems,
):
    pairs = ((nodes_hbm, nodes), (inputs_hbm, inputs), (basis_hbm, basis), (transfer_hbm, transfer))
    copies = [pltpu.make_async_copy(a, b, sems.at[i]) for i, (a, b) in enumerate(pairs)]
    for copy in copies:
        copy.start()
    for copy in copies:
        copy.wait()
    leaves = transfer.shape[0]
    size = nodes.shape[1] // leaves
    half = HALO * size
    scaled = (nodes[3:4, :] * SQLAM * inputs[...].astype(f32)).astype(bf16)
    x, y, z = nodes[0:1, :], nodes[1:2, :], nodes[2:3, :]
    centre = []
    for c, row in enumerate((x, y, z)):
        low, high = jnp.min(row), jnp.max(row)
        box[c] = low
        box[3 + c] = high
        box[6 + c] = low + 0.5 * (high - low)
        centre.append(low + 0.5 * (high - low))
    hi, mid, low = pieces(nodes[...])
    points = jnp.concatenate(
        [hi[0:3], mid[0:3], low[0:3], jnp.zeros((7, nodes.shape[1]), f32)], axis=0
    ).astype(bf16)
    stack = []
    for t in range(leaves):
        part = slice(t * size, (t + 1) * size)
        stack.append(
            lax.dot_general(
                basis[:, part], inputs[:, part], NT, preferred_element_type=f32
            ).astype(bf16)
        )
    stacked = jnp.concatenate(stack, axis=0)
    lifts = transfer[...].reshape(-1, transfer.shape[2])
    m0 = lax.dot_general(lifts, stacked, TN, preferred_element_type=f32).astype(bf16)
    moment[...] = m0
    rank = m0.shape[0]
    rhs = scaled.shape[0]
    odd = (dev[0] & 1) == 1
    low, high = slice(0, half), slice(nodes.shape[1] - half, None)
    for out, flip in ((to_chip, odd), (to_next, jnp.logical_not(odd))):
        out[0:rhs, 0:half] = jnp.where(flip, scaled[:, low], scaled[:, high])
        out[rhs : rhs + 16, 0:half] = jnp.where(flip, points[:, low], points[:, high])
        out[0:rank, half : half + 128] = jnp.concatenate([m0, jnp.zeros_like(m0)], axis=1)
        out[rhs : rhs + 16, half : half + 128] = jnp.zeros((16, 128), bf16)
    xc, yc, zc = x - centre[0], y - centre[1], z - centre[2]
    row_feat = row_features(xc, yc, zc).astype(bf16)
    col_feat = column_features(xc, yc, zc)
    for t in range(leaves):
        part = slice(t * size, (t + 1) * size)
        v_own[t] = scaled[:, part]
        rows[t] = row_feat[:, part]
        cols[t] = jnp.transpose(col_feat[:, part]).astype(bf16)
        own_xyz[t] = jnp.concatenate([nodes[:, part], jnp.zeros((4, size), f32)], axis=0)


def build_lists(dev, near_cols, near_count, inner, outer, counts):
    leaves, slots = near_cols.shape
    base = dev[0] * leaves - HALO
    dump = leaves
    lanes = inner.shape[1]
    pairs = leaves * leaves
    local = (near_cols[...] - base).astype(f32).astype(bf16)
    live = near_count[...].astype(f32).astype(bf16)
    lane = lax.broadcasted_iota(jnp.int32, (leaves, pairs), 1)
    sub = lax.broadcasted_iota(jnp.int32, (leaves, pairs), 0)
    of_t = (lane // leaves == sub).astype(f32).astype(bf16)
    of_s = (lane % leaves == sub).astype(f32).astype(bf16)
    row = lax.broadcasted_iota(jnp.int32, (1, pairs), 1)
    t_row, s_row = (row // leaves).astype(f32), (row % leaves).astype(f32)
    slot = lax.broadcasted_iota(jnp.int32, (slots, pairs), 0).astype(f32)

    def uses(spread, partner):
        cols = lax.dot_general(local, spread, TN, preferred_element_type=f32)
        count = lax.dot_general(live, spread, TN, preferred_element_type=f32)
        hit = (cols == partner) & (slot < count)
        return jnp.sum(hit.astype(f32), axis=0, keepdims=True)

    to_t = uses(of_t, s_row + HALO)
    to_s = uses(of_s, t_row + HALO)
    to_s = jnp.where(s_row > t_row, to_s, 0.0)
    to_t = jnp.where(s_row >= t_row, to_t, 0.0)
    beyond = uses(of_t, jnp.where(s_row < HALO, s_row, s_row + leaves))
    before = (
        lax.broadcasted_iota(jnp.int32, (pairs, pairs), 0)
        < lax.broadcasted_iota(jnp.int32, (pairs, pairs), 1)
    ).astype(f32).astype(bf16)
    place = lax.broadcasted_iota(jnp.int32, (lanes, pairs), 0).astype(f32) - 1.0
    where = lax.broadcasted_iota(jnp.int32, (1, lanes), 1).astype(f32) - 1.0
    for k, (out, one, two) in enumerate(((inner, to_t, to_s), (outer, beyond, None))):
        times = one if two is None else jnp.maximum(one, two)
        first = jnp.dot(times.astype(bf16), before, preferred_element_type=f32)
        mine = ((place >= first) & (place < first + times)).astype(f32).astype(bf16)
        zero = jnp.zeros_like(one)
        values = jnp.concatenate(
            [t_row, s_row, one, zero if two is None else two, first, zero, zero, zero], axis=0
        )
        got = lax.dot_general(values.astype(bf16), mine, NT, preferred_element_type=f32)
        t, s = got[0:1].astype(jnp.int32), got[1:2].astype(jnp.int32)
        nth = where - got[4:5]
        da = jnp.where(nth < got[2:3], t, dump)
        db = jnp.where(nth < got[3:4], s, dump)
        da = jnp.where(got[2:3] + got[3:4] > 0.0, da, dump)
        db = jnp.where(got[2:3] + got[3:4] > 0.0, db, dump)
        out[...] = t | s << 5 | da << 10 | db << 15
        counts[k] = jnp.sum(times).astype(jnp.int32)


def receive_halo(dev, devices, box, chip, beside, v_halo, rows, xyz, wide):
    size = v_halo.shape[2]
    rhs = v_halo.shape[1]
    half = HALO * size
    extent = [box[c] for c in range(6)]
    odd = dev[0] & 1
    edge = (dev[0] == 0) | (dev[0] == devices - 1)
    for src, side, there in ((chip, 1 - odd, dev[0] >= 0), (beside, odd, jnp.logical_not(edge))):
        pts = src[rhs : rhs + 16, 0:half].astype(f32)
        xyzs = []
        for c in range(3):
            p = pts[c : c + 1] + pts[c + 3 : c + 4] + pts[c + 6 : c + 7]
            p = jnp.where(there, p, box[6 + c])
            extent[c] = jnp.minimum(extent[c], jnp.min(p))
            extent[3 + c] = jnp.maximum(extent[3 + c], jnp.max(p))
            xyzs.append(p)
        feat = row_features(*[p - box[6 + c] for c, p in enumerate(xyzs)]).astype(bf16)
        full = jnp.concatenate([*xyzs, jnp.zeros((5, half), f32)], axis=0)
        for k in range(HALO):
            part = slice(k * size, (k + 1) * size)
            v_halo[side * HALO + k] = src[0:rhs, part]
            rows[side * HALO + k] = feat[:, part]
            xyz[side * HALO + k] = full[:, part]
    for c in range(6):
        wide[c] = extent[c]


def near_piece(
    which, lo_part, hi_part, parts, first, mutual,
    counts, todo, box, cols, rows, v_col, v_row, xyz_col, xyz_row, *rest,
):
    acc, tile_q, tile_f = rest[-3:]
    n = counts[which]
    steps = (n + UNROLL - 1) // UNROLL
    start = steps * lo_part // parts * UNROLL
    stop = jnp.minimum(steps * hi_part // parts * UNROLL, n)
    size = cols.shape[1]

    if first:
        acc[...] = jnp.zeros_like(acc)

    def entry(i):
        return todo[0, i + 1]

    def distances(code, slot):
        half = size // 2
        for r in (0, half):
            tile_q[slot, r : r + half] = jnp.dot(
                cols[code & 31, r : r + half], rows[(code >> 5) & 31], preferred_element_type=f32
            )

    def kernel_values(slot):
        for r in range(0, size, 64):
            part = tile_q[slot, r : r + 64]
            s = part + (MU - LAM * CORE2)
            p = ((s * s + A2) * s + A1) * s + A0
            tile_f[slot, r : r + 64] = ((p * p - 1.0) * lax.rsqrt(part)).astype(bf16)

    def apply(code, slot):
        t, s = code & 31, (code >> 5) & 31
        to_t, to_s = (code >> 10) & 31, (code >> 15) & 31
        acc[to_t] += lax.dot_general(v_row[s], tile_f[slot], NT, preferred_element_type=f32)
        if mutual:
            acc[to_s] += jnp.dot(v_col[t], tile_f[slot], preferred_element_type=f32)

    extent = [box[3 + c] - box[c] for c in range(3)]
    small = extent[0] * extent[0] + extent[1] * extent[1] + extent[2] * extent[2] <= RANGE2

    @pl.when(small & (stop > start))
    def _():
        tile_f[1] = jnp.zeros_like(tile_f[1])
        distances(entry(start), 0)

        def step(i, _):
            base = start + i * UNROLL
            for j in range(UNROLL):
                a, b = j % 2, 1 - j % 2
                apply(entry(base + j - 1), b)
                kernel_values(a)
                distances(entry(base + j + 1), b)
            return 0

        lax.fori_loop(0, (stop - start + UNROLL - 1) // UNROLL, step, 0)
        last = start + (stop - start + UNROLL - 1) // UNROLL * UNROLL - 1
        apply(entry(last), (UNROLL - 1) % 2)

    @pl.when(jnp.logical_not(small))
    def _():
        def step(i, _):
            code = entry(i)
            t, s = code & 31, (code >> 5) & 31
            here, there = xyz_col[t], xyz_row[s]
            squared = jnp.zeros((size, size), f32)
            for c in range(3):
                along = jnp.transpose(jnp.broadcast_to(here[c : c + 1], (size, size)))
                spread = along - there[c : c + 1]
                squared = squared + spread * spread
            tile_q[0] = squared
            for r in range(0, size, 8):
                part = tile_q[0, r : r + 8]
                tile_q[1, r : r + 8] = (
                    jnp.cos(WAVE * jnp.sqrt(part)) * lax.rsqrt(part + CORE2) * (1.0 / SQLAM)
                )
            tile_f[0] = tile_q[1].astype(bf16)
            apply(code, 0)
            return 0

        lax.fori_loop(start, stop, step, 0)


def mm(a, b):
    return jnp.dot(a, b, preferred_element_type=f32)


def lift(pair, even, odd):
    out = lax.dot_general(pair[0], even, TN, preferred_element_type=f32)
    out = out + lax.dot_general(pair[1], odd, TN, preferred_element_type=f32)
    return out.astype(bf16)


def first_step(dev, upper, moment, chip, out):
    rank, rhs = moment.shape
    half = chip.shape[1] - 128
    odd = (dev[0] & 1) == 1
    m0, other = moment[...], chip[0:rank, half : half + rhs]
    pair = (jnp.where(odd, other, m0), jnp.where(odd, m0, other))
    out[0], out[1] = pair
    if out.shape[0] > 2:
        out[2] = lift((upper[0, 0, 0], upper[0, 0, 1]), *pair)


def blocks(step):
    return 4 * (step - 1)


def join(step, low, own, got, levels):
    edges = []
    for b in range(min(step, levels)):
        k = 4 * b
        right = k + 2 if b < step - 1 else k
        edges.append((
            [jnp.where(low, own[k + i], got[k + i]) for i in range(2)],
            [jnp.where(low, got[right + i], own[right + i]) for i in range(2)],
        ))
    return edges


def next_step(step, levels, last, dev, upper, own, got, out):
    low = ((dev[0] >> step) & 1) == 0
    k = 0
    keep_left = ((dev[0] >> (step + 1)) & 1) == 1
    for left, right in join(step, low, own, got, levels):
        if last:
            for lv, rv in zip(left, right):
                out[k] = jnp.where(keep_left, lv, rv)
                k += 1
        else:
            for value in (*left, *right):
                out[k] = value
                k += 1
    if step < levels:
        m = blocks(step) + 2
        pair = (jnp.where(low, own[m], got[m]), jnp.where(low, got[m], own[m]))
        out[k], out[k + 1] = pair
        k += 2
        if k < out.shape[0]:
            out[k] = lift((upper[step, 0, 0], upper[step, 0, 1]), *pair)


def finish(top, levels, has_upper, refs):
    dev, upper, coupling, transfer, basis, acc = refs[:6]
    own = refs[6 : 6 + top]
    got = refs[6 + top : 6 + 2 * top]
    out = refs[-1]
    d = dev[0]
    zero = jnp.zeros(own[0].shape[1:], bf16)
    lefts = [[zero, zero] for _ in range(levels)]
    rights = [[zero, zero] for _ in range(levels)]
    for step in range(1, top + 1):
        mine, theirs = own[step - 1], got[step - 1]
        low = ((d >> step) & 1) == 0
        for b in range(min(step, levels)):
            count = step - 1 - b
            inner = (d >> (b + 1)) & ((1 << count) - 1)
            at_right = low & (inner == (1 << count) - 1)
            at_left = jnp.logical_not(low) & (inner == 0)
            if step == top and top > 1:
                lk = rk = 2 * b
            else:
                lk = 4 * b
                rk = lk + 2 if b < step - 1 else lk
            for i in range(2):
                rights[b][i] = jnp.where(at_right, theirs[lk + i], rights[b][i])
                lefts[b][i] = jnp.where(at_left, theirs[rk + i], lefts[b][i])
    terms = []
    for b in range(levels):
        odd = ((d >> b) & 1) == 1
        middle = jnp.where(odd, lefts[b][1], rights[b][0])
        terms.append(
            mm(coupling[b, 0, 0], lefts[b][0])
            + mm(coupling[b, 0, 1], middle)
            + mm(coupling[b, 0, 2], rights[b][1])
        )
    coeffs = terms[levels - 1]
    for b in range(has_upper - 1, -1, -1):
        coeffs = terms[b] + mm(upper[b, 0, (d >> b) & 1], coeffs.astype(bf16))
    words = coeffs.astype(bf16)
    leaves, rank, _ = transfer.shape
    leaf_coef = mm(transfer[...].reshape(leaves * rank, -1), words).astype(bf16)
    size = acc.shape[2]
    for t in range(leaves):
        part = slice(t * size, (t + 1) * size)
        far = lax.dot_general(
            leaf_coef[t * rank : (t + 1) * rank], basis[:, part], TN, preferred_element_type=f32
        )
        out[:, part] = (acc[t] + far).astype(bf16)


def on_device(devices, nodes, inputs, basis, transfer, upper, coupling, near_cols, near_count):
    leaves, rank, _ = transfer.shape
    rhs = inputs.shape[0]
    size = nodes.shape[1] // leaves
    half = HALO * size
    levels, ups = coupling.shape[0], upper.shape[0]
    dev = lax.axis_index("leaf").astype(jnp.int32).reshape(1)
    S = jax.ShapeDtypeStruct

    to_chip, to_next, v_own, rows, cols, own_xyz, box, moment = call(
        prepare, "prepare",
        (S((rhs + 16, half + 128), bf16), S((rhs + 16, half + 128), bf16), S((leaves, rhs, size), bf16),
         S((leaves, KF, size), bf16), S((leaves, size, KF), bf16), S((leaves, 8, size), f32),
         S((9,), f32), S((rank, rhs), bf16)),
        [SM] + [HBM] * 4, (VM, VM, VM, VM, VM, VM, SM, VM),
        [pltpu.VMEM(nodes.shape, f32), pltpu.VMEM(inputs.shape, bf16), pltpu.VMEM(basis.shape, bf16),
         pltpu.VMEM(transfer.shape, bf16), pltpu.SemaphoreType.DMA((4,))], us=2,
    )(dev, nodes, inputs, basis, transfer)
    chip = lax.ppermute(to_chip, "leaf", [(i, i ^ 1) for i in range(devices)])
    beside = lax.ppermute(
        to_next, "leaf",
        [p for i in range(1, devices - 1, 2) for p in ((i, i + 1), (i + 1, i))],
    )

    inner, outer, counts = call(
        build_lists, "build_lists",
        (S((1, LIST), jnp.int32), S((1, LIST), jnp.int32), S((2,), jnp.int32)),
        [SM, VM, VM], (VM, VM, SM), us=1,
    )(dev, near_cols, near_count.reshape(leaves, 1))

    scratch = [pltpu.VMEM((2, size, size), f32), pltpu.VMEM((2, size, size), bf16)]
    acc_shape = S((leaves + 1, rhs, size), f32)
    near_in = [SM, SM, SM] + [VM] * 6

    def inner_piece(lo, hi, parts, acc=None):
        args = (counts, inner, box, cols, rows, v_own, v_own, own_xyz, own_xyz)
        body = functools.partial(near_piece, 0, lo, hi, parts, acc is None, True)
        more = () if acc is None else (acc,)
        return call(
            body, f"near_inner_{lo}", acc_shape, near_in + [VM] * len(more), VM, scratch,
            {9: 0} if more else None, us=4,
        )(*args, *more)

    def outer_piece(lo, hi, parts, acc):
        return call(
            functools.partial(near_piece, 1, lo, hi, parts, False, False), f"near_outer_{lo}", acc_shape,
            near_in + [VM], VM, scratch, {9: 0}, us=4,
        )(counts, outer, wide, cols, halo_rows, v_own, v_halo, own_xyz, halo_xyz, acc)

    acc = inner_piece(0, 1, 2)

    top = devices.bit_length() - 2

    def sent(step):
        if step == top and top > 1:
            return 2 * min(step, levels)
        return 4 * (step - 1) + 2 + (1 if step <= ups else 0)

    moment, chip, acc = lax.optimization_barrier((moment, chip, acc))
    own = call(
        first_step, "first_step", S((sent(1), rank, rhs), bf16), [SM, VM, VM, VM], VM
    )(dev, upper, moment, chip)
    owns, gots = [], []
    for step in range(1, top + 1):
        got = lax.ppermute(own, "leaf", [(i, i ^ (1 << step)) for i in range(devices)])
        if step == 1:
            v_halo, halo_rows, halo_xyz, wide = call(
                lambda d, *refs: receive_halo(d, devices, *refs), "receive_halo",
                (S((2 * HALO, rhs, size), bf16), S((2 * HALO, KF, size), bf16),
                 S((2 * HALO, 8, size), f32), S((6,), f32)),
                [SM, SM, VM, VM], (VM, VM, VM, SM),
            )(dev, box, chip, beside)
        if step <= 2:
            acc = inner_piece(step + 1, step + 2, 4, acc)
        elif step <= 4:
            acc = outer_piece(step - 3, step - 2, 2, acc)
        own, got, acc = lax.optimization_barrier((own, got, acc))
        owns.append(own)
        gots.append(got)
        if step < top:
            last = step + 1 == top
            own = call(
                functools.partial(next_step, step, levels, last), "next_step",
                S((sent(step + 1), rank, rhs), bf16), [SM, VM, VM, VM], VM,
            )(dev, upper, own, got)

    return call(
        lambda *refs: finish(top, levels, ups, refs), "finish", S((rhs, leaves * size), bf16),
        [SM] + [VM] * (5 + 2 * top), VM, us=2,
    )(dev, upper, coupling, transfer, basis, acc, *owns, *gots)


def solution(mesh):
    placed = (
        P(None, "leaf"),
        P(None, "leaf"),
        P(None, "leaf"),
        P("leaf", None, None),
        P(None, "leaf", None, None, None),
        P(None, "leaf", None, None, None),
        P("leaf", None),
        P("leaf"),
    )
    return jax.shard_map(
        functools.partial(on_device, mesh.shape["leaf"]),
        mesh=mesh, in_specs=placed, out_specs=P(None, "leaf"), check_vma=False,
    )
```

```python
import functools

import jax
import jax.numpy as jnp
from jax import lax
from jax.experimental import pallas as pl
from jax.experimental.pallas import tpu as pltpu
from jax.sharding import PartitionSpec as P

f32 = jnp.float32
bf16 = jnp.bfloat16
HALO = 8
WAVE = 2.0
CORE2 = 0.05 * 0.05

RANGE2 = 4.5
LAM = 0.07457663918345607
MU = -1.1742618906652897
A2, A1, A0 = 2.3170164265523123, 2.436862577578775, -0.8205262732930618
SQLAM = LAM**0.5
BFMAX = 3.3895e38
KF = 48
UNROLL = 8
FIRST, NEXT = 1, 5
BESIDE = 2
LIST = 256
SMALL, INNER, CHIP, COUNT = 252, 253, 254, 255
NT = (((1,), (1,)), ((), ()))
TN = (((0,), (0,)), ((), ()))
NN = (((1,), (0,)), ((), ()))

VM = pl.BlockSpec(memory_space=pltpu.VMEM)
SM = pl.BlockSpec(memory_space=pltpu.SMEM)
HBM = pl.BlockSpec(memory_space=pltpu.HBM)


def call(body, name, outs, specs_in, specs_out, scratch=(), aliases=None, us=1.0, vmem=16):
    return pl.pallas_call(
        body,
        name=name,
        out_shape=outs,
        in_specs=specs_in,
        out_specs=specs_out,
        scratch_shapes=list(scratch),
        input_output_aliases=aliases or {},
        compiler_params=pltpu.CompilerParams(vmem_limit_bytes=vmem << 20),
        cost_estimate=pl.CostEstimate(
            flops=int(us * 1e9), bytes_accessed=int(us * 1e6), transcendentals=0
        ),
    )


def in_hbm(x):
    return pltpu.with_memory_space_constraint(x, pltpu.HBM)


def pieces(x):
    hi = jnp.clip(x, -BFMAX, BFMAX).astype(bf16).astype(f32)
    mid = (x - hi).astype(bf16).astype(f32)
    low = (x - hi - mid).astype(bf16).astype(f32)
    return hi, mid, low


def row_features(x, y, z):
    n = LAM * (x * x + y * y + z * z)
    one = jnp.ones_like(x)
    zero = jnp.zeros_like(x)
    hi, mid, low = pieces(jnp.concatenate([x, y, z, n, one, zero, zero, zero], axis=0))
    return jnp.concatenate([hi, mid, hi, low, hi, mid], axis=0)


def column_features(x, y, z):
    n = LAM * (x * x + y * y + z * z + CORE2)
    one = jnp.ones_like(x)
    zero = jnp.zeros_like(x)
    k = -2.0 * LAM
    hi, mid, low = pieces(
        jnp.concatenate([k * x, k * y, k * z, one, n, zero, zero, zero], axis=0)
    )
    return jnp.concatenate([hi, hi, mid, hi, low, mid], axis=0)


def write_box(box, lows, highs, centre):
    for k, value in enumerate((*lows, *highs, *centre)):
        box[k : k + 1] = jnp.broadcast_to(value, (1, box.shape[1]))


def is_small(low, high):
    extent = [b - a for a, b in zip(low, high)]
    total = extent[0] * extent[0] + extent[1] * extent[1] + extent[2] * extent[2]
    return (total <= RANGE2).astype(jnp.int32)


def prepare(
    dev, nodes_hbm, inputs_hbm, basis_hbm, transfer_hbm, cols_hbm, count_hbm,
    to_chip, to_next, v_all, rows, cols, all_xyz, box, moment, todo,
    nodes, inputs, basis, transfer, near_cols, near_count, sems,
):
    pairs = (
        (cols_hbm, near_cols), (count_hbm, near_count), (nodes_hbm, nodes), (inputs_hbm, inputs),
        (basis_hbm, basis), (transfer_hbm, transfer),
    )
    copies = [pltpu.make_async_copy(a, b, sems.at[i]) for i, (a, b) in enumerate(pairs)]
    for copy in copies:
        copy.start()
    for copy in copies[:2]:
        copy.wait()
    entries = build_list(dev[0], near_cols[...], near_count[...], 0)
    for copy in copies[2:]:
        copy.wait()
    leaves = transfer.shape[0]
    size = nodes.shape[1] // leaves
    half = HALO * size
    scaled = (nodes[3:4, :] * SQLAM * inputs[...].astype(f32)).astype(bf16)
    x, y, z = nodes[0:1, :], nodes[1:2, :], nodes[2:3, :]
    lows = [jnp.min(row, axis=1, keepdims=True) for row in (x, y, z)]
    highs = [jnp.max(row, axis=1, keepdims=True) for row in (x, y, z)]
    centre = [low + 0.5 * (high - low) for low, high in zip(lows, highs)]
    write_box(box, lows, highs, centre)
    lanes = lax.broadcasted_iota(jnp.int32, entries.shape, 1)
    todo[...] = jnp.where(lanes == SMALL, is_small(lows, highs), entries)
    hi, mid, low = pieces(nodes[...])
    points = jnp.concatenate(
        [hi[0:3], mid[0:3], low[0:3], jnp.zeros((7, nodes.shape[1]), f32)], axis=0
    ).astype(bf16)
    stack = []
    for t in range(leaves):
        part = slice(t * size, (t + 1) * size)
        stack.append(
            lax.dot_general(
                basis[:, part], inputs[:, part], NT, preferred_element_type=f32
            ).astype(bf16)
        )
    stacked = jnp.concatenate(stack, axis=0)
    lifts = transfer[...].reshape(-1, transfer.shape[2])
    m0 = lax.dot_general(lifts, stacked, TN, preferred_element_type=f32).astype(bf16)
    moment[...] = m0
    rank = m0.shape[0]
    rhs = scaled.shape[0]
    odd = (dev[0] & 1) == 1
    low, high = slice(0, half), slice(nodes.shape[1] - half, None)
    for out, flip in ((to_chip, odd), (to_next, jnp.logical_not(odd))):
        out[0:rhs, 0:half] = jnp.where(flip, scaled[:, low], scaled[:, high])
        out[rhs : rhs + 16, 0:half] = jnp.where(flip, points[:, low], points[:, high])
    to_chip[0:rank, half : half + 128] = jnp.concatenate([m0, jnp.zeros_like(m0)], axis=1)
    to_chip[rhs : rhs + 16, half : half + 128] = jnp.zeros((16, 128), bf16)
    xc, yc, zc = x - centre[0], y - centre[1], z - centre[2]
    row_feat = row_features(xc, yc, zc).astype(bf16)
    col_feat = column_features(xc, yc, zc)
    for t in range(leaves):
        part = slice(t * size, (t + 1) * size)
        v_all[t] = scaled[:, part]
        rows[t] = row_feat[:, part]
        cols[t] = jnp.transpose(col_feat[:, part]).astype(bf16)
        all_xyz[t] = jnp.concatenate([nodes[:, part], jnp.zeros((4, size), f32)], axis=0)


def build_list(dev, near_cols, near_count, small):
    leaves, slots = near_cols.shape
    base = dev * leaves - HALO
    dump = leaves
    pairs = leaves * leaves
    local = (near_cols - base).astype(f32).astype(bf16)
    live = near_count.astype(f32).astype(bf16)
    lane = lax.broadcasted_iota(jnp.int32, (leaves, pairs), 1)
    sub = lax.broadcasted_iota(jnp.int32, (leaves, pairs), 0)
    of_t = (lane // leaves == sub).astype(f32).astype(bf16)
    of_s = (lane % leaves == sub).astype(f32).astype(bf16)
    row = lax.broadcasted_iota(jnp.int32, (1, pairs), 1)
    t_row, s_row = (row // leaves).astype(f32), (row % leaves).astype(f32)
    slot = lax.broadcasted_iota(jnp.int32, (slots, pairs), 0).astype(f32)

    def slots_of(spread):
        cols = lax.dot_general(local, spread, TN, preferred_element_type=f32)
        count = lax.dot_general(live, spread, NN, preferred_element_type=f32)
        return cols, slot < count

    def uses(cols, counted, partner):
        return jnp.sum(((cols == partner) & counted).astype(f32), axis=0, keepdims=True)

    slots_t, slots_s = slots_of(of_t), slots_of(of_s)
    zero = jnp.zeros((1, pairs), f32)
    within = jnp.where(s_row >= t_row, uses(*slots_t, s_row + HALO), 0.0)
    back = jnp.where(s_row > t_row, uses(*slots_s, t_row + HALO), 0.0)
    chip_left = (dev & 1) == 1
    h_row = jnp.where(chip_left == (t_row < HALO), t_row % HALO, t_row % HALO + HALO)
    beyond = uses(*slots_s, jnp.where(h_row < HALO, h_row, h_row + leaves))
    to_t = jnp.concatenate([within, beyond], axis=1)
    to_s = jnp.concatenate([back, zero], axis=1)
    t_all = jnp.concatenate([t_row, s_row], axis=1)
    s_all = jnp.concatenate([s_row, h_row + leaves], axis=1)
    times = jnp.maximum(to_t, to_s)
    before = (
        lax.broadcasted_iota(jnp.int32, (2 * pairs, 2 * pairs), 0)
        < lax.broadcasted_iota(jnp.int32, (2 * pairs, 2 * pairs), 1)
    ).astype(f32).astype(bf16)
    first = jnp.dot(times.astype(bf16), before, preferred_element_type=f32)
    place = lax.broadcasted_iota(jnp.int32, (LIST, 2 * pairs), 0).astype(f32) - 1.0
    mine = ((place >= first) & (place < first + times)).astype(f32).astype(bf16)
    none = jnp.zeros_like(times)
    values = jnp.concatenate([t_all, s_all, to_t, to_s, first, none, none, none], axis=0)
    got = lax.dot_general(values.astype(bf16), mine, NT, preferred_element_type=f32)
    lanes = lax.broadcasted_iota(jnp.int32, (1, LIST), 1)
    nth = lanes.astype(f32) - 1.0 - got[4:5]
    t, s = got[0:1].astype(jnp.int32), got[1:2].astype(jnp.int32)
    taken = got[2:3] + got[3:4] > 0.0
    da = jnp.where(taken & (nth < got[2:3]), t, dump)
    db = jnp.where(taken & (nth < got[3:4]), s, dump)
    entries = t | s << 5 | da << 10 | db << 15
    count = jnp.sum(times, axis=1, keepdims=True).astype(jnp.int32)
    ahead = pairs + HALO * leaves
    chip = jnp.sum(times[:, :ahead], axis=1, keepdims=True).astype(jnp.int32)
    inner = jnp.sum(times[:, :pairs], axis=1, keepdims=True).astype(jnp.int32)
    for at, value in ((COUNT, count), (CHIP, chip), (INNER, inner), (SMALL, small)):
        entries = jnp.where(lanes == at, value, entries)
    return entries


def receive(on_chip, devices, dev, box, src, listed, v_all, rows, xyz, todo, wide, fetch):
    own = v_all.shape[0] - 2 * HALO
    size = v_all.shape[2]
    rhs = v_all.shape[1]
    half = HALO * size
    odd = dev[0] & 1
    side = 1 - odd if on_chip else odd
    edge = (dev[0] == 0) | (dev[0] == devices - 1)
    pts = src[rhs : rhs + 16, 0:half].astype(f32)
    coords, low, high = [], [], []
    centre = [box[6 + c : 7 + c, 0:1] for c in range(3)]
    for c in range(3):
        p = pts[c : c + 1] + pts[c + 3 : c + 4] + pts[c + 6 : c + 7]
        if not on_chip:
            p = jnp.where(edge, centre[c], p)
        low.append(jnp.minimum(box[c : c + 1, 0:1], jnp.min(p, axis=1, keepdims=True)))
        high.append(jnp.maximum(box[3 + c : 4 + c, 0:1], jnp.max(p, axis=1, keepdims=True)))
        coords.append(p)
    write_box(wide, low, high, centre)
    lane = lax.broadcasted_iota(jnp.int32, listed.shape, 1)
    todo[...] = jnp.where(lane == SMALL, is_small(low, high), listed[...])
    fetch.start()
    feat = row_features(*[p - c for p, c in zip(coords, centre)]).astype(bf16)
    full = jnp.concatenate([*coords, jnp.zeros((5, half), f32)], axis=0)
    for k in range(HALO):
        part = slice(k * size, (k + 1) * size)
        at = own + side * HALO + k
        v_all[at] = src[0:rhs, part]
        rows[at] = feat[:, part]
        xyz[at] = full[:, part]
    fetch.wait()


def near_piece(bounds, first, on_chip, devices, *refs):
    tile_q, tile_f, todo, sem = refs[-4:]
    if on_chip is None:
        listed, cols, rows, v_all, xyz = refs[:5]
        acc = refs[-5]
        fetch = pltpu.make_async_copy(listed, todo, sem)
        fetch.start()
        if first:
            acc[...] = jnp.zeros_like(acc)
        fetch.wait()
    else:
        dev, box, src, listed, cols = refs[:5]
        v_all, rows, xyz, acc, listed_out, wide = refs[-10:-4]
        fetch = pltpu.make_async_copy(listed_out, todo, sem)
        receive(on_chip, devices, dev, box, src, listed, v_all, rows, xyz, listed_out, wide, fetch)
    small = todo[0, SMALL] != 0
    n = todo[0, COUNT]
    steps = (n + UNROLL - 1) // UNROLL
    lo, hi = bounds(todo[0, INNER] // UNROLL, todo[0, CHIP] // UNROLL, steps)
    size = cols.shape[1]

    def entry(i):
        return todo[0, i + 1]

    def distances(code, slot):
        tile_q[slot] = jnp.dot(
            cols[code & 31], rows[(code >> 5) & 31], preferred_element_type=f32
        )

    def kernel_values(slot):
        for r in range(0, size, 64):
            part = tile_q[slot, r : r + 64]
            s = part + (MU - LAM * CORE2)
            p = ((s * s + A2) * s + A1) * s + A0
            tile_f[slot, r : r + 64] = ((p * p - 1.0) * lax.rsqrt(part)).astype(bf16)

    def apply(code, slot):
        t, s = code & 31, (code >> 5) & 31
        to_t, to_s = (code >> 10) & 31, (code >> 15) & 31
        acc[to_t] += lax.dot_general(v_all[s], tile_f[slot], NT, preferred_element_type=f32)
        acc[to_s] += jnp.dot(v_all[t], tile_f[slot], preferred_element_type=f32)

    @pl.when(small & (hi > lo))
    def _():
        tile_f[1] = jnp.zeros_like(tile_f[1])
        distances(entry(lo * UNROLL), 0)

        def step(i, _):
            base = i * UNROLL
            for j in range(UNROLL):
                a, b = j % 2, 1 - j % 2
                distances(entry(base + j + 1), b)
                kernel_values(a)
                apply(entry(base + j - 1), b)
            return 0

        lax.fori_loop(lo, hi, step, 0)
        apply(entry(hi * UNROLL - 1), (UNROLL - 1) % 2)

    @pl.when(jnp.logical_not(small))
    def _():
        def step(i, _):
            code = entry(i)
            t, s = code & 31, (code >> 5) & 31
            here, there = xyz[t], xyz[s]
            squared = jnp.zeros((size, size), f32)
            for c in range(3):
                along = jnp.transpose(jnp.broadcast_to(here[c : c + 1], (size, size)))
                spread = along - there[c : c + 1]
                squared = squared + spread * spread
            tile_q[0] = squared
            for r in range(0, size, 8):
                part = tile_q[0, r : r + 8]
                tile_q[1, r : r + 8] = (
                    jnp.cos(WAVE * jnp.sqrt(part)) * lax.rsqrt(part + CORE2) * (1.0 / SQLAM)
                )
            tile_f[0] = tile_q[1].astype(bf16)
            apply(code, 0)
            return 0

        lax.fori_loop(lo * UNROLL, jnp.minimum(hi * UNROLL, n), step, 0)


def mm(a, b):
    return jnp.dot(a, b, preferred_element_type=f32)


def lift(pair, even, odd):
    out = lax.dot_general(pair[0], even, TN, preferred_element_type=f32)
    out = out + lax.dot_general(pair[1], odd, TN, preferred_element_type=f32)
    return out.astype(bf16)


def first_step(dev, upper, moment, chip, out):
    rank, rhs = moment.shape
    half = chip.shape[1] - 128
    odd = (dev[0] & 1) == 1
    m0, other = moment[...], chip[0:rank, half : half + rhs]
    pair = (jnp.where(odd, other, m0), jnp.where(odd, m0, other))
    out[0], out[1] = pair
    out[2] = lift((upper[0, 0, 0], upper[0, 0, 1]), *pair)


def next_step(step, dev, upper, own, got, out):
    k = 2 * step
    low = ((dev[0] >> step) & 1) == 0
    pair = (jnp.where(low, own[k], got[k]), jnp.where(low, got[k], own[k]))
    if out.shape[0] == 2:
        out[0], out[1] = pair
        return
    out[0:k] = own[0:k]
    out[k], out[k + 1] = pair
    out[k + 2] = lift((upper[step, 0, 0], upper[step, 0, 1]), *pair)


def finish(levels, has_upper, refs):
    dev, upper, coupling, transfer, basis, acc = refs[:6]
    gots = refs[6:-4]
    middle = refs[-4]
    out, held, sems = refs[-3:]
    d = dev[0]
    terms = []
    for b in range(levels):
        zero = jnp.zeros(gots[0].shape[1:], bf16)
        left, right = [zero, zero], [zero, zero]
        for step in range(b + 1, len(gots) + 1):
            got, k = gots[step - 1], 2 * b
            if step == len(gots):
                got, k = (got, 0) if b == step - 1 else (middle, k)
            low = ((d >> step) & 1) == 0
            full = (1 << (step - 1 - b)) - 1
            inner = (d >> (b + 1)) & full
            before = jnp.logical_not(low) & (inner == 0)
            after = low & (inner == full)
            for i in range(2):
                left[i] = jnp.where(before, got[k + i], left[i])
                right[i] = jnp.where(after, got[k + i], right[i])
        crossed = jnp.where(((d >> b) & 1) == 1, left[1], right[0])
        terms.append(
            mm(coupling[b, 0, 0], left[0])
            + mm(coupling[b, 0, 1], crossed)
            + mm(coupling[b, 0, 2], right[1])
        )
    coeffs = terms[levels - 1]
    for b in range(has_upper - 1, -1, -1):
        coeffs = terms[b] + mm(upper[b, 0, (d >> b) & 1], coeffs.astype(bf16))
    words = coeffs.astype(bf16)
    leaves, rank, _ = transfer.shape
    leaf_coef = mm(transfer[...].reshape(leaves * rank, -1), words).astype(bf16)
    size = acc.shape[2]
    copies = []
    for t in range(leaves):
        part = slice(t * size, (t + 1) * size)
        far = lax.dot_general(
            leaf_coef[t * rank : (t + 1) * rank], basis[:, part], TN, preferred_element_type=f32
        )
        held[:, part] = (acc[t] + far).astype(bf16)
        if (t + 1) % 4 == 0:
            done = pl.ds((t - 3) * size, 4 * size)
            copies.append(pltpu.make_async_copy(held.at[:, done], out.at[:, done], sems.at[t // 4]))
            copies[-1].start()
    for copy in copies:
        copy.wait()


def on_device(devices, nodes, inputs, basis, transfer, upper, coupling, near_cols, near_count):
    leaves, rank, _ = transfer.shape
    rhs = inputs.shape[0]
    size = nodes.shape[1] // leaves
    half = HALO * size
    levels, ups = coupling.shape[0], upper.shape[0]
    dev = lax.axis_index("leaf").astype(jnp.int32).reshape(1)
    S = jax.ShapeDtypeStruct

    to_chip, to_next, v_all, rows, cols, xyz, box, moment, todo = call(
        prepare, "prepare",
        (S((rhs + 16, half + 128), bf16), S((rhs + 16, half), bf16),
         S((leaves + 2 * HALO, rhs, size), bf16), S((leaves + 2 * HALO, KF, size), bf16),
         S((leaves, size, KF), bf16), S((leaves + 2 * HALO, 8, size), f32),
         S((16, 128), f32), S((rank, rhs), bf16), S((1, LIST), jnp.int32)),
        [SM] + [HBM] * 6, (VM,) * 9,
        [pltpu.VMEM(nodes.shape, f32), pltpu.VMEM(inputs.shape, bf16), pltpu.VMEM(basis.shape, bf16),
         pltpu.VMEM(transfer.shape, bf16), pltpu.VMEM(near_cols.shape, jnp.int32),
         pltpu.VMEM((1, leaves), jnp.int32), pltpu.SemaphoreType.DMA((6,))], us=2,
    )(dev, *map(in_hbm, (nodes, inputs, basis, transfer, near_cols, near_count.reshape(1, leaves))))
    chip = lax.ppermute(to_chip, "leaf", [(i, i ^ 1) for i in range(devices)])
    acc_shape = S((leaves + 1, rhs, size), f32)

    scratch = [
        pltpu.VMEM((2, size, size), f32), pltpu.VMEM((2, size, size), bf16),
        pltpu.SMEM((1, LIST), jnp.int32), pltpu.SemaphoreType.DMA,
    ]

    def near(name, bounds, us, acc=None):
        more = () if acc is None else (acc,)
        return call(
            functools.partial(near_piece, bounds, acc is None, None, devices), name, acc_shape,
            [VM] * (5 + len(more)), VM, scratch, {5: 0} if more else None, us=us,
        )(todo, cols, rows, v_all, xyz, *more)

    def near_after(name, bounds, us, on_chip, sent, acc):
        halo = (v_all, rows, xyz, acc)
        return call(
            functools.partial(near_piece, bounds, False, on_chip, devices), name,
            (*[S(a.shape, a.dtype) for a in halo], S(todo.shape, jnp.int32), S(box.shape, f32)),
            [SM] + [VM] * 8, (VM,) * 6, scratch, {5: 0, 6: 1, 7: 2, 8: 3}, us=us,
        )(dev, box, sent, todo, cols, *halo)

    def upto(k):
        return lambda inner, chip: jnp.minimum(jnp.minimum(FIRST, inner) + k * NEXT, chip)

    first = lambda inner, chip, steps: (0, jnp.minimum(FIRST, inner))
    pieces_of = [
        lambda inner, chip, steps: (upto(0)(inner, chip), upto(1)(inner, chip)),
        lambda inner, chip, steps: (upto(1)(inner, chip), upto(2)(inner, chip)),
        lambda inner, chip, steps: (upto(2)(inner, chip), chip),
        lambda inner, chip, steps: (chip, steps),
    ]
    halves = {1: (True, "chip"), 4: (False, "beside")}
    acc = near("near_0", first, 2)
    acc, chip, moment = lax.optimization_barrier((acc, chip, moment))

    def block_count(step):
        return 2 if step == levels else 2 * step + 1

    own = call(
        first_step, "first_step", S((block_count(1), rank, rhs), bf16), [SM, VM, VM, VM], VM
    )(dev, upper, moment, chip)
    own, chip = lax.optimization_barrier((own, chip))
    gots = []
    for step in range(1, levels + 1):
        mirror = (2 << step) - 2
        got = lax.ppermute(own, "leaf", [(i, i ^ mirror) for i in range(devices)])
        if step == levels:
            acc, beside = lax.optimization_barrier((acc, beside))
        if step in (1, levels):
            sent = chip if step == 1 else beside
            v_all, rows, xyz, acc, todo, box = near_after(f"near_{step}", pieces_of[min(step, 4) - 1], 4, step == 1, sent, acc)
        elif step < 4:
            acc = near(f"near_{step}", pieces_of[step - 1], 3, acc)
        if step == BESIDE:
            to_next, acc = lax.optimization_barrier((to_next, acc))
            beside = lax.ppermute(
                to_next, "leaf",
                [p for i in range(1, devices - 1, 2) for p in ((i, i + 1), (i + 1, i))],
            )
        if step == levels - 1:
            sent, acc = lax.optimization_barrier((own, acc))
            middle = lax.ppermute(
                sent, "leaf",
                [(i, i ^ (devices - 2)) for i in range(devices // 4, 3 * devices // 4)],
            )
        own, got, acc = lax.optimization_barrier((own, got, acc))
        if step < levels:
            own = call(
                functools.partial(next_step, step), "next_step",
                S((block_count(step + 1), rank, rhs), bf16), [SM, VM, VM, VM], VM,
            )(dev, upper, own, got)
            own, acc = lax.optimization_barrier((own, acc))
        gots.append(got)
    gots.append(middle)

    return call(
        lambda *refs: finish(levels, ups, refs), "finish", S((rhs, leaves * size), bf16),
        [SM] + [VM] * (5 + len(gots)), HBM,
        [pltpu.VMEM((rhs, leaves * size), bf16), pltpu.SemaphoreType.DMA((leaves // 4,))], us=2,
    )(dev, upper, coupling, transfer, basis, acc, *gots)


def solution(mesh):
    placed = (
        P(None, "leaf"),
        P(None, "leaf"),
        P(None, "leaf"),
        P("leaf", None, None),
        P(None, "leaf", None, None, None),
        P(None, "leaf", None, None, None),
        P("leaf", None),
        P("leaf"),
    )
    return jax.shard_map(
        functools.partial(on_device, mesh.shape["leaf"]),
        mesh=mesh, in_specs=placed, out_specs=P(None, "leaf"), check_vma=False,
    )
```

```python
import functools

import jax
import jax.numpy as jnp
from jax import lax
from jax.experimental import pallas as pl
from jax.experimental.pallas import tpu as pltpu
from jax.sharding import PartitionSpec as P

f32 = jnp.float32
bf16 = jnp.bfloat16
HALO = 8
WAVE = 2.0
CORE2 = 0.05 * 0.05

RANGE2 = 4.5
LAM0, MU0 = 0.07457663918345607, -1.1742618906652897
A2, A1, A0 = 2.3170164265523123, 2.436862577578775, -0.8205262732930618
G = A1 ** (-1.0 / 3.0)
LAM, MU = G * LAM0, G * MU0
SHIFT = MU - LAM * CORE2
B2, B0 = G**2 * A2, G**4 * A0
LAST = B0 * B0 - G**8
SCALE = G**8 / LAM**0.5
BFMAX = 3.3895e38
KF = 48
UNROLL = 8
FIRST, NEXT = 1, 5
BESIDE = 2
LIST = 256
SMALL, INNER, CHIP, COUNT = 252, 253, 254, 255
NT = (((1,), (1,)), ((), ()))
TN = (((0,), (0,)), ((), ()))
NN = (((1,), (0,)), ((), ()))

VM = pl.BlockSpec(memory_space=pltpu.VMEM)
SM = pl.BlockSpec(memory_space=pltpu.SMEM)
HBM = pl.BlockSpec(memory_space=pltpu.HBM)


def call(body, name, outs, specs_in, specs_out, scratch=(), aliases=None, us=1.0, vmem=16):
    return pl.pallas_call(
        body,
        name=name,
        out_shape=outs,
        in_specs=specs_in,
        out_specs=specs_out,
        scratch_shapes=list(scratch),
        input_output_aliases=aliases or {},
        compiler_params=pltpu.CompilerParams(vmem_limit_bytes=vmem << 20),
        cost_estimate=pl.CostEstimate(
            flops=int(us * 1e9), bytes_accessed=int(us * 1e6), transcendentals=0
        ),
    )


def in_hbm(x):
    return pltpu.with_memory_space_constraint(x, pltpu.HBM)


def pieces(x):
    hi = jnp.clip(x, -BFMAX, BFMAX).astype(bf16).astype(f32)
    mid = (x - hi).astype(bf16).astype(f32)
    low = (x - hi - mid).astype(bf16).astype(f32)
    return hi, mid, low


def row_features(x, y, z):
    n = LAM * (x * x + y * y + z * z)
    one = jnp.ones_like(x)
    zero = jnp.zeros_like(x)
    hi, mid, low = pieces(jnp.concatenate([x, y, z, n, one, zero, zero, zero], axis=0))
    return jnp.concatenate([hi, mid, hi, low, hi, mid], axis=0)


def column_features(x, y, z):
    n = LAM * (x * x + y * y + z * z + CORE2)
    one = jnp.ones_like(x)
    zero = jnp.zeros_like(x)
    k = -2.0 * LAM
    hi, mid, low = pieces(
        jnp.concatenate([k * x, k * y, k * z, one, n, zero, zero, zero], axis=0)
    )
    return jnp.concatenate([hi, hi, mid, hi, low, mid], axis=0)


def write_box(box, lows, highs, centre):
    for k, value in enumerate((*lows, *highs, *centre)):
        box[k : k + 1] = jnp.broadcast_to(value, (1, box.shape[1]))


def is_small(low, high):
    extent = [b - a for a, b in zip(low, high)]
    total = extent[0] * extent[0] + extent[1] * extent[1] + extent[2] * extent[2]
    return (total <= RANGE2).astype(jnp.int32)


def prepare(
    dev, nodes_hbm, inputs_hbm, basis_hbm, transfer_hbm, cols_hbm, count_hbm,
    to_chip, to_next, v_all, rows, cols, all_xyz, box, moment, todo,
    nodes, inputs, basis, transfer, near_cols, near_count, sems,
):
    pairs = (
        (cols_hbm, near_cols), (count_hbm, near_count), (nodes_hbm, nodes), (inputs_hbm, inputs),
        (basis_hbm, basis), (transfer_hbm, transfer),
    )
    copies = [pltpu.make_async_copy(a, b, sems.at[i]) for i, (a, b) in enumerate(pairs)]
    for copy in copies:
        copy.start()
    for copy in copies[:2]:
        copy.wait()
    entries = build_list(dev[0], near_cols[...], near_count[...], 0)
    for copy in copies[2:]:
        copy.wait()
    leaves = transfer.shape[0]
    size = nodes.shape[1] // leaves
    half = HALO * size
    scaled = (nodes[3:4, :] * (1.0 / SCALE) * inputs[...].astype(f32)).astype(bf16)
    x, y, z = nodes[0:1, :], nodes[1:2, :], nodes[2:3, :]
    lows = [jnp.min(row, axis=1, keepdims=True) for row in (x, y, z)]
    highs = [jnp.max(row, axis=1, keepdims=True) for row in (x, y, z)]
    centre = [low + 0.5 * (high - low) for low, high in zip(lows, highs)]
    write_box(box, lows, highs, centre)
    lanes = lax.broadcasted_iota(jnp.int32, entries.shape, 1)
    todo[...] = jnp.where(lanes == SMALL, is_small(lows, highs), entries)
    hi, mid, low = pieces(nodes[...])
    points = jnp.concatenate(
        [hi[0:3], mid[0:3], low[0:3], jnp.zeros((7, nodes.shape[1]), f32)], axis=0
    ).astype(bf16)
    stack = []
    for t in range(leaves):
        part = slice(t * size, (t + 1) * size)
        stack.append(
            lax.dot_general(
                basis[:, part], inputs[:, part], NT, preferred_element_type=f32
            ).astype(bf16)
        )
    stacked = jnp.concatenate(stack, axis=0)
    lifts = transfer[...].reshape(-1, transfer.shape[2])
    m0 = lax.dot_general(lifts, stacked, TN, preferred_element_type=f32).astype(bf16)
    moment[...] = m0
    rank = m0.shape[0]
    rhs = scaled.shape[0]
    odd = (dev[0] & 1) == 1
    low, high = slice(0, half), slice(nodes.shape[1] - half, None)
    for out, flip in ((to_chip, odd), (to_next, jnp.logical_not(odd))):
        out[0:rhs, 0:half] = jnp.where(flip, scaled[:, low], scaled[:, high])
        out[rhs : rhs + 16, 0:half] = jnp.where(flip, points[:, low], points[:, high])
    to_chip[0:rank, half : half + 128] = jnp.concatenate([m0, jnp.zeros_like(m0)], axis=1)
    to_chip[rhs : rhs + 16, half : half + 128] = jnp.zeros((16, 128), bf16)
    xc, yc, zc = x - centre[0], y - centre[1], z - centre[2]
    row_feat = row_features(xc, yc, zc).astype(bf16)
    col_feat = column_features(xc, yc, zc)
    for t in range(leaves):
        part = slice(t * size, (t + 1) * size)
        v_all[t] = scaled[:, part]
        rows[t] = row_feat[:, part]
        cols[t] = jnp.transpose(col_feat[:, part]).astype(bf16)
        all_xyz[t] = jnp.concatenate([nodes[:, part], jnp.zeros((4, size), f32)], axis=0)


def build_list(dev, near_cols, near_count, small):
    leaves, slots = near_cols.shape
    base = dev * leaves - HALO
    dump = leaves
    pairs = leaves * leaves
    local = (near_cols - base).astype(f32).astype(bf16)
    live = near_count.astype(f32).astype(bf16)
    lane = lax.broadcasted_iota(jnp.int32, (leaves, pairs), 1)
    sub = lax.broadcasted_iota(jnp.int32, (leaves, pairs), 0)
    of_t = (lane // leaves == sub).astype(f32).astype(bf16)
    of_s = (lane % leaves == sub).astype(f32).astype(bf16)
    row = lax.broadcasted_iota(jnp.int32, (1, pairs), 1)
    t_row, s_row = (row // leaves).astype(f32), (row % leaves).astype(f32)
    slot = lax.broadcasted_iota(jnp.int32, (slots, pairs), 0).astype(f32)

    def slots_of(spread):
        cols = lax.dot_general(local, spread, TN, preferred_element_type=f32)
        count = lax.dot_general(live, spread, NN, preferred_element_type=f32)
        return cols, slot < count

    def uses(cols, counted, partner):
        return jnp.sum(((cols == partner) & counted).astype(f32), axis=0, keepdims=True)

    slots_t, slots_s = slots_of(of_t), slots_of(of_s)
    zero = jnp.zeros((1, pairs), f32)
    within = jnp.where(s_row >= t_row, uses(*slots_t, s_row + HALO), 0.0)
    back = jnp.where(s_row > t_row, uses(*slots_s, t_row + HALO), 0.0)
    chip_left = (dev & 1) == 1
    h_row = jnp.where(chip_left == (t_row < HALO), t_row % HALO, t_row % HALO + HALO)
    beyond = uses(*slots_s, jnp.where(h_row < HALO, h_row, h_row + leaves))
    to_t = jnp.concatenate([within, beyond], axis=1)
    to_s = jnp.concatenate([back, zero], axis=1)
    t_all = jnp.concatenate([t_row, s_row], axis=1)
    s_all = jnp.concatenate([s_row, h_row + leaves], axis=1)
    times = jnp.maximum(to_t, to_s)
    before = (
        lax.broadcasted_iota(jnp.int32, (2 * pairs, 2 * pairs), 0)
        < lax.broadcasted_iota(jnp.int32, (2 * pairs, 2 * pairs), 1)
    ).astype(f32).astype(bf16)
    first = jnp.dot(times.astype(bf16), before, preferred_element_type=f32)
    place = lax.broadcasted_iota(jnp.int32, (LIST, 2 * pairs), 0).astype(f32) - 1.0
    mine = ((place >= first) & (place < first + times)).astype(f32).astype(bf16)
    none = jnp.zeros_like(times)
    values = jnp.concatenate([t_all, s_all, to_t, to_s, first, none, none, none], axis=0)
    got = lax.dot_general(values.astype(bf16), mine, NT, preferred_element_type=f32)
    lanes = lax.broadcasted_iota(jnp.int32, (1, LIST), 1)
    nth = lanes.astype(f32) - 1.0 - got[4:5]
    t, s = got[0:1].astype(jnp.int32), got[1:2].astype(jnp.int32)
    taken = got[2:3] + got[3:4] > 0.0
    da = jnp.where(taken & (nth < got[2:3]), t, dump)
    db = jnp.where(taken & (nth < got[3:4]), s, dump)
    entries = t | s << 5 | da << 10 | db << 15
    count = jnp.sum(times, axis=1, keepdims=True).astype(jnp.int32)
    ahead = pairs + HALO * leaves
    chip = jnp.sum(times[:, :ahead], axis=1, keepdims=True).astype(jnp.int32)
    inner = jnp.sum(times[:, :pairs], axis=1, keepdims=True).astype(jnp.int32)
    for at, value in ((COUNT, count), (CHIP, chip), (INNER, inner), (SMALL, small)):
        entries = jnp.where(lanes == at, value, entries)
    return entries


def receive(on_chip, devices, dev, box, src, listed, v_all, rows, xyz, todo, wide, fetch):
    own = v_all.shape[0] - 2 * HALO
    size = v_all.shape[2]
    rhs = v_all.shape[1]
    half = HALO * size
    odd = dev[0] & 1
    side = 1 - odd if on_chip else odd
    edge = (dev[0] == 0) | (dev[0] == devices - 1)
    pts = src[rhs : rhs + 16, 0:half].astype(f32)
    coords, low, high = [], [], []
    centre = [box[6 + c : 7 + c, 0:1] for c in range(3)]
    for c in range(3):
        p = pts[c : c + 1] + pts[c + 3 : c + 4] + pts[c + 6 : c + 7]
        if not on_chip:
            p = jnp.where(edge, centre[c], p)
        low.append(jnp.minimum(box[c : c + 1, 0:1], jnp.min(p, axis=1, keepdims=True)))
        high.append(jnp.maximum(box[3 + c : 4 + c, 0:1], jnp.max(p, axis=1, keepdims=True)))
        coords.append(p)
    write_box(wide, low, high, centre)
    lane = lax.broadcasted_iota(jnp.int32, listed.shape, 1)
    todo[...] = jnp.where(lane == SMALL, is_small(low, high), listed[...])
    fetch.start()
    feat = row_features(*[p - c for p, c in zip(coords, centre)]).astype(bf16)
    full = jnp.concatenate([*coords, jnp.zeros((5, half), f32)], axis=0)
    for k in range(HALO):
        part = slice(k * size, (k + 1) * size)
        at = own + side * HALO + k
        v_all[at] = src[0:rhs, part]
        rows[at] = feat[:, part]
        xyz[at] = full[:, part]
    fetch.wait()


def near_piece(bounds, first, on_chip, devices, *refs):
    tile_q, tile_f, todo, sem = refs[-4:]
    if on_chip is None:
        listed, cols, rows, v_all, xyz = refs[:5]
        acc = refs[-5]
        fetch = pltpu.make_async_copy(listed, todo, sem)
        fetch.start()
        if first:
            acc[...] = jnp.zeros_like(acc)
        fetch.wait()
    else:
        dev, box, src, listed, cols = refs[:5]
        v_all, rows, xyz, acc, listed_out, wide = refs[-10:-4]
        fetch = pltpu.make_async_copy(listed_out, todo, sem)
        receive(on_chip, devices, dev, box, src, listed, v_all, rows, xyz, listed_out, wide, fetch)
    small = todo[0, SMALL] != 0
    n = todo[0, COUNT]
    steps = (n + UNROLL - 1) // UNROLL
    lo, hi = bounds(todo[0, INNER] // UNROLL, todo[0, CHIP] // UNROLL, steps)
    size = cols.shape[1]

    def entry(i):
        return todo[0, i + 1]

    def distances(code, slot):
        tile_q[slot] = jnp.dot(
            cols[code & 31], rows[(code >> 5) & 31], preferred_element_type=f32
        )

    def kernel_values(slot):
        for r in range(0, size, 64):
            part = tile_q[slot, r : r + 64]
            s = part + SHIFT
            y = s * s
            p = (y + B2) * y + s
            tile_f[slot, r : r + 64] = (((p + 2.0 * B0) * p + LAST) * lax.rsqrt(part)).astype(bf16)

    def apply(code, slot):
        t, s = code & 31, (code >> 5) & 31
        to_t, to_s = (code >> 10) & 31, (code >> 15) & 31
        acc[to_t] += lax.dot_general(v_all[s], tile_f[slot], NT, preferred_element_type=f32)
        acc[to_s] += jnp.dot(v_all[t], tile_f[slot], preferred_element_type=f32)

    @pl.when(small & (hi > lo))
    def _():
        tile_f[1] = jnp.zeros_like(tile_f[1])
        distances(entry(lo * UNROLL), 0)

        def step(i, _):
            base = i * UNROLL
            for j in range(UNROLL):
                a, b = j % 2, 1 - j % 2
                distances(entry(base + j + 1), b)
                kernel_values(a)
                apply(entry(base + j - 1), b)
            return 0

        lax.fori_loop(lo, hi, step, 0)
        apply(entry(hi * UNROLL - 1), (UNROLL - 1) % 2)

    @pl.when(jnp.logical_not(small))
    def _():
        def step(i, _):
            code = entry(i)
            t, s = code & 31, (code >> 5) & 31
            here, there = xyz[t], xyz[s]
            squared = jnp.zeros((size, size), f32)
            for c in range(3):
                along = jnp.transpose(jnp.broadcast_to(here[c : c + 1], (size, size)))
                spread = along - there[c : c + 1]
                squared = squared + spread * spread
            tile_q[0] = squared
            for r in range(0, size, 8):
                part = tile_q[0, r : r + 8]
                tile_q[1, r : r + 8] = (
                    jnp.cos(WAVE * jnp.sqrt(part)) * lax.rsqrt(part + CORE2) * SCALE
                )
            tile_f[0] = tile_q[1].astype(bf16)
            apply(code, 0)
            return 0

        lax.fori_loop(lo * UNROLL, jnp.minimum(hi * UNROLL, n), step, 0)


def mm(a, b):
    return jnp.dot(a, b, preferred_element_type=f32)


def lift(pair, even, odd):
    out = lax.dot_general(pair[0], even, TN, preferred_element_type=f32)
    out = out + lax.dot_general(pair[1], odd, TN, preferred_element_type=f32)
    return out.astype(bf16)


def first_step(dev, upper, moment, chip, out):
    rank, rhs = moment.shape
    half = chip.shape[1] - 128
    odd = (dev[0] & 1) == 1
    m0, other = moment[...], chip[0:rank, half : half + rhs]
    pair = (jnp.where(odd, other, m0), jnp.where(odd, m0, other))
    out[0], out[1] = pair
    out[2] = lift((upper[0, 0, 0], upper[0, 0, 1]), *pair)


def next_step(step, dev, upper, own, got, out):
    k = 2 * step
    low = ((dev[0] >> step) & 1) == 0
    pair = (jnp.where(low, own[k], got[k]), jnp.where(low, got[k], own[k]))
    if out.shape[0] == 2:
        out[0], out[1] = pair
        return
    out[0:k] = own[0:k]
    out[k], out[k + 1] = pair
    out[k + 2] = lift((upper[step, 0, 0], upper[step, 0, 1]), *pair)


def finish(levels, has_upper, refs):
    dev, upper, coupling, transfer, basis, acc = refs[:6]
    gots = refs[6:-4]
    middle = refs[-4]
    out, held, sems = refs[-3:]
    d = dev[0]
    terms = []
    for b in range(levels):
        zero = jnp.zeros(gots[0].shape[1:], bf16)
        left, right = [zero, zero], [zero, zero]
        for step in range(b + 1, len(gots) + 1):
            got, k = gots[step - 1], 2 * b
            if step == len(gots):
                got, k = (got, 0) if b == step - 1 else (middle, k)
            low = ((d >> step) & 1) == 0
            full = (1 << (step - 1 - b)) - 1
            inner = (d >> (b + 1)) & full
            before = jnp.logical_not(low) & (inner == 0)
            after = low & (inner == full)
            for i in range(2):
                left[i] = jnp.where(before, got[k + i], left[i])
                right[i] = jnp.where(after, got[k + i], right[i])
        crossed = jnp.where(((d >> b) & 1) == 1, left[1], right[0])
        terms.append(
            mm(coupling[b, 0, 0], left[0])
            + mm(coupling[b, 0, 1], crossed)
            + mm(coupling[b, 0, 2], right[1])
        )
    coeffs = terms[levels - 1]
    for b in range(has_upper - 1, -1, -1):
        coeffs = terms[b] + mm(upper[b, 0, (d >> b) & 1], coeffs.astype(bf16))
    words = coeffs.astype(bf16)
    leaves, rank, _ = transfer.shape
    leaf_coef = mm(transfer[...].reshape(leaves * rank, -1), words).astype(bf16)
    size = acc.shape[2]
    copies = []
    for t in range(leaves):
        part = slice(t * size, (t + 1) * size)
        far = lax.dot_general(
            leaf_coef[t * rank : (t + 1) * rank], basis[:, part], TN, preferred_element_type=f32
        )
        held[:, part] = (acc[t] + far).astype(bf16)
        if (t + 1) % 4 == 0:
            done = pl.ds((t - 3) * size, 4 * size)
            copies.append(pltpu.make_async_copy(held.at[:, done], out.at[:, done], sems.at[t // 4]))
            copies[-1].start()
    for copy in copies:
        copy.wait()


def on_device(devices, nodes, inputs, basis, transfer, upper, coupling, near_cols, near_count):
    leaves, rank, _ = transfer.shape
    rhs = inputs.shape[0]
    size = nodes.shape[1] // leaves
    half = HALO * size
    levels, ups = coupling.shape[0], upper.shape[0]
    dev = lax.axis_index("leaf").astype(jnp.int32).reshape(1)
    S = jax.ShapeDtypeStruct

    to_chip, to_next, v_all, rows, cols, xyz, box, moment, todo = call(
        prepare, "prepare",
        (S((rhs + 16, half + 128), bf16), S((rhs + 16, half), bf16),
         S((leaves + 2 * HALO, rhs, size), bf16), S((leaves + 2 * HALO, KF, size), bf16),
         S((leaves, size, KF), bf16), S((leaves + 2 * HALO, 8, size), f32),
         S((16, 128), f32), S((rank, rhs), bf16), S((1, LIST), jnp.int32)),
        [SM] + [HBM] * 6, (VM,) * 9,
        [pltpu.VMEM(nodes.shape, f32), pltpu.VMEM(inputs.shape, bf16), pltpu.VMEM(basis.shape, bf16),
         pltpu.VMEM(transfer.shape, bf16), pltpu.VMEM(near_cols.shape, jnp.int32),
         pltpu.VMEM((1, leaves), jnp.int32), pltpu.SemaphoreType.DMA((6,))], us=2,
    )(dev, *map(in_hbm, (nodes, inputs, basis, transfer, near_cols, near_count.reshape(1, leaves))))
    chip = lax.ppermute(to_chip, "leaf", [(i, i ^ 1) for i in range(devices)])
    acc_shape = S((leaves + 1, rhs, size), f32)

    scratch = [
        pltpu.VMEM((2, size, size), f32), pltpu.VMEM((2, size, size), bf16),
        pltpu.SMEM((1, LIST), jnp.int32), pltpu.SemaphoreType.DMA,
    ]

    def near(name, bounds, us, acc=None):
        more = () if acc is None else (acc,)
        return call(
            functools.partial(near_piece, bounds, acc is None, None, devices), name, acc_shape,
            [VM] * (5 + len(more)), VM, scratch, {5: 0} if more else None, us=us,
        )(todo, cols, rows, v_all, xyz, *more)

    def near_after(name, bounds, us, on_chip, sent, acc):
        halo = (v_all, rows, xyz, acc)
        return call(
            functools.partial(near_piece, bounds, False, on_chip, devices), name,
            (*[S(a.shape, a.dtype) for a in halo], S(todo.shape, jnp.int32), S(box.shape, f32)),
            [SM] + [VM] * 8, (VM,) * 6, scratch, {5: 0, 6: 1, 7: 2, 8: 3}, us=us,
        )(dev, box, sent, todo, cols, *halo)

    def upto(k):
        return lambda inner, chip: jnp.minimum(jnp.minimum(FIRST, inner) + k * NEXT, chip)

    first = lambda inner, chip, steps: (0, jnp.minimum(FIRST, inner))
    pieces_of = [
        lambda inner, chip, steps: (upto(0)(inner, chip), upto(1)(inner, chip)),
        lambda inner, chip, steps: (upto(1)(inner, chip), upto(2)(inner, chip)),
        lambda inner, chip, steps: (upto(2)(inner, chip), chip),
        lambda inner, chip, steps: (chip, steps),
    ]
    halves = {1: (True, "chip"), 4: (False, "beside")}
    acc = near("near_0", first, 2)
    acc, chip, moment = lax.optimization_barrier((acc, chip, moment))

    def block_count(step):
        return 2 if step == levels else 2 * step + 1

    own = call(
        first_step, "first_step", S((block_count(1), rank, rhs), bf16), [SM, VM, VM, VM], VM
    )(dev, upper, moment, chip)
    own, chip = lax.optimization_barrier((own, chip))
    gots = []
    for step in range(1, levels + 1):
        mirror = (2 << step) - 2
        got = lax.ppermute(own, "leaf", [(i, i ^ mirror) for i in range(devices)])
        if step == levels:
            acc, beside = lax.optimization_barrier((acc, beside))
        if step in (1, levels):
            sent = chip if step == 1 else beside
            v_all, rows, xyz, acc, todo, box = near_after(f"near_{step}", pieces_of[min(step, 4) - 1], 4, step == 1, sent, acc)
        elif step < 4:
            acc = near(f"near_{step}", pieces_of[step - 1], 3, acc)
        if step == BESIDE:
            to_next, acc = lax.optimization_barrier((to_next, acc))
            beside = lax.ppermute(
                to_next, "leaf",
                [p for i in range(1, devices - 1, 2) for p in ((i, i + 1), (i + 1, i))],
            )
        if step == levels - 1:
            sent, acc = lax.optimization_barrier((own, acc))
            middle = lax.ppermute(
                sent, "leaf",
                [(i, i ^ (devices - 2)) for i in range(devices // 4, 3 * devices // 4)],
            )
        own, got, acc = lax.optimization_barrier((own, got, acc))
        if step < levels:
            own = call(
                functools.partial(next_step, step), "next_step",
                S((block_count(step + 1), rank, rhs), bf16), [SM, VM, VM, VM], VM,
            )(dev, upper, own, got)
            own, acc = lax.optimization_barrier((own, acc))
        gots.append(got)
    gots.append(middle)

    return call(
        lambda *refs: finish(levels, ups, refs), "finish", S((rhs, leaves * size), bf16),
        [SM] + [VM] * (5 + len(gots)), HBM,
        [pltpu.VMEM((rhs, leaves * size), bf16), pltpu.SemaphoreType.DMA((leaves // 4,))], us=2,
    )(dev, upper, coupling, transfer, basis, acc, *gots)


def solution(mesh):
    placed = (
        P(None, "leaf"),
        P(None, "leaf"),
        P(None, "leaf"),
        P("leaf", None, None),
        P(None, "leaf", None, None, None),
        P(None, "leaf", None, None, None),
        P("leaf", None),
        P("leaf"),
    )
    return jax.shard_map(
        functools.partial(on_device, mesh.shape["leaf"]),
        mesh=mesh, in_specs=placed, out_specs=P(None, "leaf"), check_vma=False,
    )
```

```python
import functools

import jax
import jax.numpy as jnp
from jax import lax
from jax.experimental import pallas as pl
from jax.experimental.pallas import tpu as pltpu
from jax.sharding import PartitionSpec as P

f32 = jnp.float32
bf16 = jnp.bfloat16
HALO = 8
WAVE = 2.0
CORE2 = 0.05 * 0.05

RANGE2 = 4.5
LAM0, MU0 = 0.07457663918345607, -1.1742618906652897
A2, A1, A0 = 2.3170164265523123, 2.436862577578775, -0.8205262732930618
G = A1 ** (-1.0 / 3.0)
LAM, MU = G * LAM0, G * MU0
SHIFT = MU - LAM * CORE2
B2, B0 = G**2 * A2, G**4 * A0
LAST = B0 * B0 - G**8
SCALE = G**8 / LAM**0.5
BFMAX = 3.3895e38
KF = 48
UNROLL = 8
FIRST, NEXT = 1, 4
BESIDE = 2
LIST = 256
SMALL, INNER, CHIP, COUNT = 252, 253, 254, 255
NT = (((1,), (1,)), ((), ()))
TN = (((0,), (0,)), ((), ()))
NN = (((1,), (0,)), ((), ()))

VM = pl.BlockSpec(memory_space=pltpu.VMEM)
SM = pl.BlockSpec(memory_space=pltpu.SMEM)
HBM = pl.BlockSpec(memory_space=pltpu.HBM)


def call(body, name, outs, specs_in, specs_out, scratch=(), aliases=None, us=1.0, vmem=16):
    return pl.pallas_call(
        body,
        name=name,
        out_shape=outs,
        in_specs=specs_in,
        out_specs=specs_out,
        scratch_shapes=list(scratch),
        input_output_aliases=aliases or {},
        compiler_params=pltpu.CompilerParams(vmem_limit_bytes=vmem << 20),
        cost_estimate=pl.CostEstimate(
            flops=int(us * 1e9), bytes_accessed=int(us * 1e6), transcendentals=0
        ),
    )


def in_hbm(x):
    return pltpu.with_memory_space_constraint(x, pltpu.HBM)


def pieces(x):
    hi = jnp.clip(x, -BFMAX, BFMAX).astype(bf16).astype(f32)
    mid = (x - hi).astype(bf16).astype(f32)
    low = (x - hi - mid).astype(bf16).astype(f32)
    return hi, mid, low


def row_features(x, y, z):
    n = LAM * (x * x + y * y + z * z)
    one = jnp.ones_like(x)
    zero = jnp.zeros_like(x)
    hi, mid, low = pieces(jnp.concatenate([x, y, z, n, one, zero, zero, zero], axis=0))
    return jnp.concatenate([hi, mid, hi, low, hi, mid], axis=0)


def column_features(x, y, z):
    n = LAM * (x * x + y * y + z * z + CORE2)
    one = jnp.ones_like(x)
    zero = jnp.zeros_like(x)
    k = -2.0 * LAM
    hi, mid, low = pieces(
        jnp.concatenate([k * x, k * y, k * z, one, n, zero, zero, zero], axis=0)
    )
    return jnp.concatenate([hi, hi, mid, hi, low, mid], axis=0)


def write_box(box, lows, highs, centre):
    for k, value in enumerate((*lows, *highs, *centre)):
        box[k : k + 1] = jnp.broadcast_to(value, (1, box.shape[1]))


def is_small(low, high):
    extent = [b - a for a, b in zip(low, high)]
    total = extent[0] * extent[0] + extent[1] * extent[1] + extent[2] * extent[2]
    return (total <= RANGE2).astype(jnp.int32)


def prepare(
    dev, nodes_hbm, inputs_hbm, basis_hbm, transfer_hbm, cols_hbm, count_hbm,
    to_chip, to_next, v_all, rows, cols, all_xyz, box, moment, todo,
    nodes, inputs, basis, transfer, near_cols, near_count, sems,
):
    pairs = (
        (cols_hbm, near_cols), (count_hbm, near_count), (nodes_hbm, nodes), (inputs_hbm, inputs),
        (basis_hbm, basis), (transfer_hbm, transfer),
    )
    copies = [pltpu.make_async_copy(a, b, sems.at[i]) for i, (a, b) in enumerate(pairs)]
    for copy in copies:
        copy.start()
    for copy in copies[:2]:
        copy.wait()
    entries = build_list(dev[0], near_cols[...], near_count[...], 0)
    for copy in copies[2:]:
        copy.wait()
    leaves = transfer.shape[0]
    size = nodes.shape[1] // leaves
    half = HALO * size
    scaled = (nodes[3:4, :] * (1.0 / SCALE) * inputs[...].astype(f32)).astype(bf16)
    x, y, z = nodes[0:1, :], nodes[1:2, :], nodes[2:3, :]
    lows = [jnp.min(row, axis=1, keepdims=True) for row in (x, y, z)]
    highs = [jnp.max(row, axis=1, keepdims=True) for row in (x, y, z)]
    centre = [low + 0.5 * (high - low) for low, high in zip(lows, highs)]
    write_box(box, lows, highs, centre)
    lanes = lax.broadcasted_iota(jnp.int32, entries.shape, 1)
    todo[...] = jnp.where(lanes == SMALL, is_small(lows, highs), entries)
    hi, mid, low = pieces(nodes[...])
    points = jnp.concatenate(
        [hi[0:3], mid[0:3], low[0:3], jnp.zeros((7, nodes.shape[1]), f32)], axis=0
    ).astype(bf16)
    stack = []
    for t in range(leaves):
        part = slice(t * size, (t + 1) * size)
        stack.append(
            lax.dot_general(
                basis[:, part], inputs[:, part], NT, preferred_element_type=f32
            ).astype(bf16)
        )
    stacked = jnp.concatenate(stack, axis=0)
    lifts = transfer[...].reshape(-1, transfer.shape[2])
    m0 = lax.dot_general(lifts, stacked, TN, preferred_element_type=f32).astype(bf16)
    moment[...] = m0
    rank = m0.shape[0]
    rhs = scaled.shape[0]
    odd = (dev[0] & 1) == 1
    low, high = slice(0, half), slice(nodes.shape[1] - half, None)
    for out, flip in ((to_chip, odd), (to_next, jnp.logical_not(odd))):
        out[0:rhs, 0:half] = jnp.where(flip, scaled[:, low], scaled[:, high])
        out[rhs : rhs + 16, 0:half] = jnp.where(flip, points[:, low], points[:, high])
    to_chip[0:rank, half : half + 128] = jnp.concatenate([m0, jnp.zeros_like(m0)], axis=1)
    to_chip[rhs : rhs + 16, half : half + 128] = jnp.zeros((16, 128), bf16)
    xc, yc, zc = x - centre[0], y - centre[1], z - centre[2]
    row_feat = row_features(xc, yc, zc).astype(bf16)
    col_feat = column_features(xc, yc, zc)
    for t in range(leaves):
        part = slice(t * size, (t + 1) * size)
        v_all[t] = scaled[:, part]
        rows[t] = row_feat[:, part]
        cols[t] = jnp.transpose(col_feat[:, part]).astype(bf16)
        all_xyz[t] = jnp.concatenate([nodes[:, part], jnp.zeros((4, size), f32)], axis=0)


def build_list(dev, near_cols, near_count, small):
    leaves, slots = near_cols.shape
    base = dev * leaves - HALO
    dump = leaves
    pairs = leaves * leaves
    local = (near_cols - base).astype(f32).astype(bf16)
    live = near_count.astype(f32).astype(bf16)
    lane = lax.broadcasted_iota(jnp.int32, (leaves, pairs), 1)
    sub = lax.broadcasted_iota(jnp.int32, (leaves, pairs), 0)
    of_t = (lane // leaves == sub).astype(f32).astype(bf16)
    of_s = (lane % leaves == sub).astype(f32).astype(bf16)
    row = lax.broadcasted_iota(jnp.int32, (1, pairs), 1)
    t_row, s_row = (row // leaves).astype(f32), (row % leaves).astype(f32)
    slot = lax.broadcasted_iota(jnp.int32, (slots, pairs), 0).astype(f32)

    def slots_of(spread):
        cols = lax.dot_general(local, spread, TN, preferred_element_type=f32)
        count = lax.dot_general(live, spread, NN, preferred_element_type=f32)
        return cols, slot < count

    def uses(cols, counted, partner):
        return jnp.sum(((cols == partner) & counted).astype(f32), axis=0, keepdims=True)

    slots_t, slots_s = slots_of(of_t), slots_of(of_s)
    zero = jnp.zeros((1, pairs), f32)
    within = jnp.where(s_row >= t_row, uses(*slots_t, s_row + HALO), 0.0)
    back = jnp.where(s_row > t_row, uses(*slots_s, t_row + HALO), 0.0)
    chip_left = (dev & 1) == 1
    h_row = jnp.where(chip_left == (t_row < HALO), t_row % HALO, t_row % HALO + HALO)
    beyond = uses(*slots_s, jnp.where(h_row < HALO, h_row, h_row + leaves))
    to_t = jnp.concatenate([within, beyond], axis=1)
    to_s = jnp.concatenate([back, zero], axis=1)
    t_all = jnp.concatenate([t_row, s_row], axis=1)
    s_all = jnp.concatenate([s_row, h_row + leaves], axis=1)
    times = jnp.maximum(to_t, to_s)
    before = (
        lax.broadcasted_iota(jnp.int32, (2 * pairs, 2 * pairs), 0)
        < lax.broadcasted_iota(jnp.int32, (2 * pairs, 2 * pairs), 1)
    ).astype(f32).astype(bf16)
    first = jnp.dot(times.astype(bf16), before, preferred_element_type=f32)
    place = lax.broadcasted_iota(jnp.int32, (LIST, 2 * pairs), 0).astype(f32) - 1.0
    mine = ((place >= first) & (place < first + times)).astype(f32).astype(bf16)
    none = jnp.zeros_like(times)
    values = jnp.concatenate([t_all, s_all, to_t, to_s, first, none, none, none], axis=0)
    got = lax.dot_general(values.astype(bf16), mine, NT, preferred_element_type=f32)
    lanes = lax.broadcasted_iota(jnp.int32, (1, LIST), 1)
    nth = lanes.astype(f32) - 1.0 - got[4:5]
    t, s = got[0:1].astype(jnp.int32), got[1:2].astype(jnp.int32)
    taken = got[2:3] + got[3:4] > 0.0
    da = jnp.where(taken & (nth < got[2:3]), t, dump)
    db = jnp.where(taken & (nth < got[3:4]), s, dump)
    entries = t | s << 5 | da << 10 | db << 15
    count = jnp.sum(times, axis=1, keepdims=True).astype(jnp.int32)
    ahead = pairs + HALO * leaves
    chip = jnp.sum(times[:, :ahead], axis=1, keepdims=True).astype(jnp.int32)
    inner = jnp.sum(times[:, :pairs], axis=1, keepdims=True).astype(jnp.int32)
    for at, value in ((COUNT, count), (CHIP, chip), (INNER, inner), (SMALL, small)):
        entries = jnp.where(lanes == at, value, entries)
    return entries


def receive(on_chip, devices, dev, box, src, listed, v_all, rows, xyz, todo, wide, fetch):
    own = v_all.shape[0] - 2 * HALO
    size = v_all.shape[2]
    rhs = v_all.shape[1]
    half = HALO * size
    odd = dev[0] & 1
    side = 1 - odd if on_chip else odd
    edge = (dev[0] == 0) | (dev[0] == devices - 1)
    pts = src[rhs : rhs + 16, 0:half].astype(f32)
    coords, low, high = [], [], []
    centre = [box[6 + c : 7 + c, 0:1] for c in range(3)]
    for c in range(3):
        p = pts[c : c + 1] + pts[c + 3 : c + 4] + pts[c + 6 : c + 7]
        if not on_chip:
            p = jnp.where(edge, centre[c], p)
        low.append(jnp.minimum(box[c : c + 1, 0:1], jnp.min(p, axis=1, keepdims=True)))
        high.append(jnp.maximum(box[3 + c : 4 + c, 0:1], jnp.max(p, axis=1, keepdims=True)))
        coords.append(p)
    write_box(wide, low, high, centre)
    lane = lax.broadcasted_iota(jnp.int32, listed.shape, 1)
    todo[...] = jnp.where(lane == SMALL, is_small(low, high), listed[...])
    fetch.start()
    feat = row_features(*[p - c for p, c in zip(coords, centre)]).astype(bf16)
    full = jnp.concatenate([*coords, jnp.zeros((5, half), f32)], axis=0)
    for k in range(HALO):
        part = slice(k * size, (k + 1) * size)
        at = own + side * HALO + k
        v_all[at] = src[0:rhs, part]
        rows[at] = feat[:, part]
        xyz[at] = full[:, part]
    fetch.wait()


def near_piece(bounds, first, on_chip, devices, *refs):
    tile_q, tile_f, todo, sem = refs[-4:]
    if on_chip is None:
        listed, cols, rows, v_all, xyz = refs[:5]
        acc = refs[-5]
        fetch = pltpu.make_async_copy(listed, todo, sem)
        fetch.start()
        if first:
            acc[...] = jnp.zeros_like(acc)
        fetch.wait()
    else:
        dev, box, src, listed, cols = refs[:5]
        v_all, rows, xyz, acc, listed_out, wide = refs[-10:-4]
        fetch = pltpu.make_async_copy(listed_out, todo, sem)
        receive(on_chip, devices, dev, box, src, listed, v_all, rows, xyz, listed_out, wide, fetch)
    small = todo[0, SMALL] != 0
    n = todo[0, COUNT]
    steps = (n + UNROLL - 1) // UNROLL
    lo, hi = bounds(todo[0, INNER] // UNROLL, todo[0, CHIP] // UNROLL, steps)
    size = cols.shape[1]

    def entry(i):
        return todo[0, i + 1]

    def distances(code, slot):
        tile_q[slot] = jnp.dot(
            cols[code & 31], rows[(code >> 5) & 31], preferred_element_type=f32
        )

    def kernel_values(slot):
        for r in range(0, size, 64):
            part = tile_q[slot, r : r + 64]
            s = part + SHIFT
            y = s * s
            p = (y + B2) * y + s
            tile_f[slot, r : r + 64] = (((p + 2.0 * B0) * p + LAST) * lax.rsqrt(part)).astype(bf16)

    def apply(code, slot):
        t, s = code & 31, (code >> 5) & 31
        to_t, to_s = (code >> 10) & 31, (code >> 15) & 31
        acc[to_t] += lax.dot_general(v_all[s], tile_f[slot], NT, preferred_element_type=f32)
        acc[to_s] += jnp.dot(v_all[t], tile_f[slot], preferred_element_type=f32)

    @pl.when(small & (hi > lo))
    def _():
        tile_f[1] = jnp.zeros_like(tile_f[1])
        distances(entry(lo * UNROLL), 0)

        def step(i, _):
            base = i * UNROLL
            for j in range(UNROLL):
                a, b = j % 2, 1 - j % 2
                distances(entry(base + j + 1), b)
                kernel_values(a)
                apply(entry(base + j - 1), b)
            return 0

        lax.fori_loop(lo, hi, step, 0)
        apply(entry(hi * UNROLL - 1), (UNROLL - 1) % 2)

    @pl.when(jnp.logical_not(small))
    def _():
        def step(i, _):
            code = entry(i)
            t, s = code & 31, (code >> 5) & 31
            here, there = xyz[t], xyz[s]
            squared = jnp.zeros((size, size), f32)
            for c in range(3):
                along = jnp.transpose(jnp.broadcast_to(here[c : c + 1], (size, size)))
                spread = along - there[c : c + 1]
                squared = squared + spread * spread
            tile_q[0] = squared
            for r in range(0, size, 8):
                part = tile_q[0, r : r + 8]
                tile_q[1, r : r + 8] = (
                    jnp.cos(WAVE * jnp.sqrt(part)) * lax.rsqrt(part + CORE2) * SCALE
                )
            tile_f[0] = tile_q[1].astype(bf16)
            apply(code, 0)
            return 0

        lax.fori_loop(lo * UNROLL, jnp.minimum(hi * UNROLL, n), step, 0)


def mm(a, b):
    return jnp.dot(a, b, preferred_element_type=f32)


def lift(pair, even, odd):
    out = lax.dot_general(pair[0], even, TN, preferred_element_type=f32)
    out = out + lax.dot_general(pair[1], odd, TN, preferred_element_type=f32)
    return out.astype(bf16)


def first_step(dev, upper, moment, chip, out):
    rank, rhs = moment.shape
    half = chip.shape[1] - 128
    odd = (dev[0] & 1) == 1
    m0, other = moment[...], chip[0:rank, half : half + rhs]
    pair = (jnp.where(odd, other, m0), jnp.where(odd, m0, other))
    out[0], out[1] = pair
    out[2] = lift((upper[0, 0, 0], upper[0, 0, 1]), *pair)


def next_step(step, dev, upper, own, got, out):
    k = 2 * step
    low = ((dev[0] >> step) & 1) == 0
    pair = (jnp.where(low, own[k], got[k]), jnp.where(low, got[k], own[k]))
    out[0:k] = own[0:k]
    out[k], out[k + 1] = pair
    if out.shape[0] > k + 2:
        out[k + 2] = lift((upper[step, 0, 0], upper[step, 0, 1]), *pair)


def finish(levels, has_upper, refs):
    dev, upper, coupling, transfer, basis, acc = refs[:6]
    gots = refs[6:-3]
    out, held, sems = refs[-3:]
    d = dev[0]
    terms = []
    for b in range(levels):
        zero = jnp.zeros(gots[0].shape[1:], bf16)
        left, right = [zero, zero], [zero, zero]
        for step in range(b + 1, len(gots) + 1):
            got, k = gots[step - 1], 2 * b
            low = ((d >> step) & 1) == 0
            full = (1 << (step - 1 - b)) - 1
            inner = (d >> (b + 1)) & full
            before = jnp.logical_not(low) & (inner == 0)
            after = low & (inner == full)
            for i in range(2):
                left[i] = jnp.where(before, got[k + i], left[i])
                right[i] = jnp.where(after, got[k + i], right[i])
        crossed = jnp.where(((d >> b) & 1) == 1, left[1], right[0])
        terms.append(
            mm(coupling[b, 0, 0], left[0])
            + mm(coupling[b, 0, 1], crossed)
            + mm(coupling[b, 0, 2], right[1])
        )
    coeffs = terms[levels - 1]
    for b in range(has_upper - 1, -1, -1):
        coeffs = terms[b] + mm(upper[b, 0, (d >> b) & 1], coeffs.astype(bf16))
    words = coeffs.astype(bf16)
    leaves, rank, _ = transfer.shape
    leaf_coef = mm(transfer[...].reshape(leaves * rank, -1), words).astype(bf16)
    size = acc.shape[2]
    copies = []
    for t in range(leaves):
        part = slice(t * size, (t + 1) * size)
        far = lax.dot_general(
            leaf_coef[t * rank : (t + 1) * rank], basis[:, part], TN, preferred_element_type=f32
        )
        held[:, part] = (acc[t] + far).astype(bf16)
        if (t + 1) % 4 == 0:
            done = pl.ds((t - 3) * size, 4 * size)
            copies.append(pltpu.make_async_copy(held.at[:, done], out.at[:, done], sems.at[t // 4]))
            copies[-1].start()
    for copy in copies:
        copy.wait()


def on_device(devices, nodes, inputs, basis, transfer, upper, coupling, near_cols, near_count):
    leaves, rank, _ = transfer.shape
    rhs = inputs.shape[0]
    size = nodes.shape[1] // leaves
    half = HALO * size
    levels, ups = coupling.shape[0], upper.shape[0]
    dev = lax.axis_index("leaf").astype(jnp.int32).reshape(1)
    S = jax.ShapeDtypeStruct

    to_chip, to_next, v_all, rows, cols, xyz, box, moment, todo = call(
        prepare, "prepare",
        (S((rhs + 16, half + 128), bf16), S((rhs + 16, half), bf16),
         S((leaves + 2 * HALO, rhs, size), bf16), S((leaves + 2 * HALO, KF, size), bf16),
         S((leaves, size, KF), bf16), S((leaves + 2 * HALO, 8, size), f32),
         S((16, 128), f32), S((rank, rhs), bf16), S((1, LIST), jnp.int32)),
        [SM] + [HBM] * 6, (VM,) * 9,
        [pltpu.VMEM(nodes.shape, f32), pltpu.VMEM(inputs.shape, bf16), pltpu.VMEM(basis.shape, bf16),
         pltpu.VMEM(transfer.shape, bf16), pltpu.VMEM(near_cols.shape, jnp.int32),
         pltpu.VMEM((1, leaves), jnp.int32), pltpu.SemaphoreType.DMA((6,))], us=2,
    )(dev, *map(in_hbm, (nodes, inputs, basis, transfer, near_cols, near_count.reshape(1, leaves))))
    chip = lax.ppermute(to_chip, "leaf", [(i, i ^ 1) for i in range(devices)])
    acc_shape = S((leaves + 1, rhs, size), f32)

    scratch = [
        pltpu.VMEM((2, size, size), f32), pltpu.VMEM((2, size, size), bf16),
        pltpu.SMEM((1, LIST), jnp.int32), pltpu.SemaphoreType.DMA,
    ]

    def near(name, bounds, us, acc=None):
        more = () if acc is None else (acc,)
        return call(
            functools.partial(near_piece, bounds, acc is None, None, devices), name, acc_shape,
            [VM] * (5 + len(more)), VM, scratch, {5: 0} if more else None, us=us,
        )(todo, cols, rows, v_all, xyz, *more)

    def near_after(name, bounds, us, on_chip, sent, acc):
        halo = (v_all, rows, xyz, acc)
        return call(
            functools.partial(near_piece, bounds, False, on_chip, devices), name,
            (*[S(a.shape, a.dtype) for a in halo], S(todo.shape, jnp.int32), S(box.shape, f32)),
            [SM] + [VM] * 8, (VM,) * 6, scratch, {5: 0, 6: 1, 7: 2, 8: 3}, us=us,
        )(dev, box, sent, todo, cols, *halo)

    def upto(k):
        return lambda inner, chip: jnp.minimum(jnp.minimum(FIRST, inner) + k * NEXT, chip)

    first = lambda inner, chip, steps: (0, jnp.minimum(FIRST, inner))
    pieces_of = [
        lambda inner, chip, steps: (upto(0)(inner, chip), upto(1)(inner, chip)),
        lambda inner, chip, steps: (upto(1)(inner, chip), upto(2)(inner, chip)),
        lambda inner, chip, steps: (upto(2)(inner, chip), chip),
        lambda inner, chip, steps: (chip, steps),
    ]
    acc = near("near_0", first, 2)
    acc, chip, moment = lax.optimization_barrier((acc, chip, moment))

    def block_count(step):
        return 2 * step + (1 if step < levels else 0)

    own = call(
        first_step, "first_step", S((block_count(1), rank, rhs), bf16), [SM, VM, VM, VM], VM
    )(dev, upper, moment, chip)
    own, chip = lax.optimization_barrier((own, chip))
    gots = []
    for step in range(1, levels + 1):
        mirror = (2 << step) - 2
        got = lax.ppermute(own, "leaf", [(i, i ^ mirror) for i in range(devices)])
        if step == levels:
            acc, beside = lax.optimization_barrier((acc, beside))
        if step in (1, levels):
            sent = chip if step == 1 else beside
            v_all, rows, xyz, acc, todo, box = near_after(f"near_{step}", pieces_of[min(step, 4) - 1], 4, step == 1, sent, acc)
        elif step < 4:
            acc = near(f"near_{step}", pieces_of[step - 1], 3, acc)
        if step == BESIDE:
            to_next, acc = lax.optimization_barrier((to_next, acc))
            beside = lax.ppermute(
                to_next, "leaf",
                [p for i in range(1, devices - 1, 2) for p in ((i, i + 1), (i + 1, i))],
            )
        own, got, acc = lax.optimization_barrier((own, got, acc))
        if step < levels:
            own = call(
                functools.partial(next_step, step), "next_step",
                S((block_count(step + 1), rank, rhs), bf16), [SM, VM, VM, VM], VM,
            )(dev, upper, own, got)
            own, acc = lax.optimization_barrier((own, acc))
        gots.append(got)

    return call(
        lambda *refs: finish(levels, ups, refs), "finish", S((rhs, leaves * size), bf16),
        [SM] + [VM] * (5 + len(gots)), HBM,
        [pltpu.VMEM((rhs, leaves * size), bf16), pltpu.SemaphoreType.DMA((leaves // 4,))], us=2,
    )(dev, upper, coupling, transfer, basis, acc, *gots)


def solution(mesh):
    placed = (
        P(None, "leaf"),
        P(None, "leaf"),
        P(None, "leaf"),
        P("leaf", None, None),
        P(None, "leaf", None, None, None),
        P(None, "leaf", None, None, None),
        P("leaf", None),
        P("leaf"),
    )
    return jax.shard_map(
        functools.partial(on_device, mesh.shape["leaf"]),
        mesh=mesh, in_specs=placed, out_specs=P(None, "leaf"), check_vma=False,
    )
```

```python
import functools

import jax
import jax.numpy as jnp
from jax import lax
from jax.experimental import pallas as pl
from jax.experimental.pallas import tpu as pltpu
from jax.sharding import PartitionSpec as P

f32 = jnp.float32
bf16 = jnp.bfloat16
HALO = 8
WAVE = 2.0
CORE2 = 0.05 * 0.05

RANGE2 = 4.5
LAM0, MU0 = 0.07457663918345607, -1.1742618906652897
A2, A1, A0 = 2.3170164265523123, 2.436862577578775, -0.8205262732930618
G = A1 ** (-1.0 / 3.0)
LAM, MU = G * LAM0, G * MU0
SHIFT = MU - LAM * CORE2
B2, B0 = G**2 * A2, G**4 * A0
LAST = B0 * B0 - G**8
SCALE = G**8 / LAM**0.5
BFMAX = 3.3895e38
KF = 48
UNROLL = 8
FIRST, NEXT = 0, 5
BESIDE = 2
LIST = 256
SMALL, INNER, CHIP, COUNT = 252, 253, 254, 255
NT = (((1,), (1,)), ((), ()))
TN = (((0,), (0,)), ((), ()))
NN = (((1,), (0,)), ((), ()))

VM = pl.BlockSpec(memory_space=pltpu.VMEM)
SM = pl.BlockSpec(memory_space=pltpu.SMEM)
HBM = pl.BlockSpec(memory_space=pltpu.HBM)


def call(body, name, outs, specs_in, specs_out, scratch=(), aliases=None, us=1.0, vmem=16):
    return pl.pallas_call(
        body,
        name=name,
        out_shape=outs,
        in_specs=specs_in,
        out_specs=specs_out,
        scratch_shapes=list(scratch),
        input_output_aliases=aliases or {},
        compiler_params=pltpu.CompilerParams(vmem_limit_bytes=vmem << 20),
        cost_estimate=pl.CostEstimate(
            flops=int(us * 1e9), bytes_accessed=int(us * 1e6), transcendentals=0
        ),
    )


def in_hbm(x):
    return pltpu.with_memory_space_constraint(x, pltpu.HBM)


def pieces(x):
    hi = jnp.clip(x, -BFMAX, BFMAX).astype(bf16).astype(f32)
    mid = (x - hi).astype(bf16).astype(f32)
    low = (x - hi - mid).astype(bf16).astype(f32)
    return hi, mid, low


def row_features(x, y, z):
    n = LAM * (x * x + y * y + z * z)
    one = jnp.ones_like(x)
    zero = jnp.zeros_like(x)
    hi, mid, low = pieces(jnp.concatenate([x, y, z, n, one, zero, zero, zero], axis=0))
    return jnp.concatenate([hi, mid, hi, low, hi, mid], axis=0)


def column_features(x, y, z):
    n = LAM * (x * x + y * y + z * z + CORE2)
    one = jnp.ones_like(x)
    zero = jnp.zeros_like(x)
    k = -2.0 * LAM
    hi, mid, low = pieces(
        jnp.concatenate([k * x, k * y, k * z, one, n, zero, zero, zero], axis=0)
    )
    return jnp.concatenate([hi, hi, mid, hi, low, mid], axis=0)


def write_box(box, lows, highs, centre):
    for k, value in enumerate((*lows, *highs, *centre)):
        box[k : k + 1] = jnp.broadcast_to(value, (1, box.shape[1]))


def is_small(low, high):
    extent = [b - a for a, b in zip(low, high)]
    total = extent[0] * extent[0] + extent[1] * extent[1] + extent[2] * extent[2]
    return (total <= RANGE2).astype(jnp.int32)


def prepare(
    dev, nodes_hbm, inputs_hbm, basis_hbm, transfer_hbm,
    to_chip, to_next, v_all, all_xyz, box, moment,
    nodes, inputs, basis, transfer, sems,
):
    pairs = (
        (nodes_hbm, nodes), (inputs_hbm, inputs),
        (basis_hbm, basis), (transfer_hbm, transfer),
    )
    copies = [pltpu.make_async_copy(a, b, sems.at[i]) for i, (a, b) in enumerate(pairs)]
    for copy in copies:
        copy.start()
    for copy in copies:
        copy.wait()
    leaves = transfer.shape[0]
    size = nodes.shape[1] // leaves
    half = HALO * size
    scaled = (nodes[3:4, :] * (1.0 / SCALE) * inputs[...].astype(f32)).astype(bf16)
    x, y, z = nodes[0:1, :], nodes[1:2, :], nodes[2:3, :]
    lows = [jnp.min(row, axis=1, keepdims=True) for row in (x, y, z)]
    highs = [jnp.max(row, axis=1, keepdims=True) for row in (x, y, z)]
    centre = [low + 0.5 * (high - low) for low, high in zip(lows, highs)]
    write_box(box, lows, highs, centre)
    hi, mid, low = pieces(nodes[...])
    points = jnp.concatenate(
        [hi[0:3], mid[0:3], low[0:3], jnp.zeros((7, nodes.shape[1]), f32)], axis=0
    ).astype(bf16)
    stack = []
    for t in range(leaves):
        part = slice(t * size, (t + 1) * size)
        stack.append(
            lax.dot_general(
                basis[:, part], inputs[:, part], NT, preferred_element_type=f32
            ).astype(bf16)
        )
    stacked = jnp.concatenate(stack, axis=0)
    lifts = transfer[...].reshape(-1, transfer.shape[2])
    m0 = lax.dot_general(lifts, stacked, TN, preferred_element_type=f32).astype(bf16)
    moment[...] = m0
    rank = m0.shape[0]
    rhs = scaled.shape[0]
    odd = (dev[0] & 1) == 1
    low, high = slice(0, half), slice(nodes.shape[1] - half, None)
    for out, flip in ((to_chip, odd), (to_next, jnp.logical_not(odd))):
        out[0:rhs, 0:half] = jnp.where(flip, scaled[:, low], scaled[:, high])
        out[rhs : rhs + 16, 0:half] = jnp.where(flip, points[:, low], points[:, high])
    to_chip[0:rank, half : half + 128] = jnp.concatenate([m0, jnp.zeros_like(m0)], axis=1)
    to_chip[rhs : rhs + 16, half : half + 128] = jnp.zeros((16, 128), bf16)
    for t in range(leaves):
        part = slice(t * size, (t + 1) * size)
        v_all[t] = scaled[:, part]
        all_xyz[t] = jnp.concatenate([nodes[:, part], jnp.zeros((4, size), f32)], axis=0)


def arrange(dev, xyz, box, near_cols, near_count, rows, cols, todo, acc):
    acc[...] = jnp.zeros_like(acc)
    low, high, centre = ([box[k + c : k + c + 1, 0:1] for c in range(3)] for k in (0, 3, 6))
    for t in range(cols.shape[0]):
        point = [xyz[t, c : c + 1] - centre[c] for c in range(3)]
        rows[t] = row_features(*point).astype(bf16)
        cols[t] = jnp.transpose(column_features(*point)).astype(bf16)
    todo[...] = build_list(dev[0], near_cols[...], near_count[...], is_small(low, high))


def build_list(dev, near_cols, near_count, small):
    leaves, slots = near_cols.shape
    base = dev * leaves - HALO
    dump = leaves
    pairs = leaves * leaves
    local = (near_cols - base).astype(f32).astype(bf16)
    live = near_count.astype(f32).astype(bf16)
    lane = lax.broadcasted_iota(jnp.int32, (leaves, pairs), 1)
    sub = lax.broadcasted_iota(jnp.int32, (leaves, pairs), 0)
    of_t = (lane // leaves == sub).astype(f32).astype(bf16)
    of_s = (lane % leaves == sub).astype(f32).astype(bf16)
    row = lax.broadcasted_iota(jnp.int32, (1, pairs), 1)
    t_row, s_row = (row // leaves).astype(f32), (row % leaves).astype(f32)
    slot = lax.broadcasted_iota(jnp.int32, (slots, pairs), 0).astype(f32)

    def slots_of(spread):
        cols = lax.dot_general(local, spread, TN, preferred_element_type=f32)
        count = lax.dot_general(live, spread, NN, preferred_element_type=f32)
        return cols, slot < count

    def uses(cols, counted, partner):
        return jnp.sum(((cols == partner) & counted).astype(f32), axis=0, keepdims=True)

    slots_t, slots_s = slots_of(of_t), slots_of(of_s)
    zero = jnp.zeros((1, pairs), f32)
    within = jnp.where(s_row >= t_row, uses(*slots_t, s_row + HALO), 0.0)
    back = jnp.where(s_row > t_row, uses(*slots_s, t_row + HALO), 0.0)
    chip_left = (dev & 1) == 1
    h_row = jnp.where(chip_left == (t_row < HALO), t_row % HALO, t_row % HALO + HALO)
    beyond = uses(*slots_s, jnp.where(h_row < HALO, h_row, h_row + leaves))
    to_t = jnp.concatenate([within, beyond], axis=1)
    to_s = jnp.concatenate([back, zero], axis=1)
    t_all = jnp.concatenate([t_row, s_row], axis=1)
    s_all = jnp.concatenate([s_row, h_row + leaves], axis=1)
    times = jnp.maximum(to_t, to_s)
    before = (
        lax.broadcasted_iota(jnp.int32, (2 * pairs, 2 * pairs), 0)
        < lax.broadcasted_iota(jnp.int32, (2 * pairs, 2 * pairs), 1)
    ).astype(f32).astype(bf16)
    first = jnp.dot(times.astype(bf16), before, preferred_element_type=f32)
    place = lax.broadcasted_iota(jnp.int32, (LIST, 2 * pairs), 0).astype(f32) - 1.0
    mine = ((place >= first) & (place < first + times)).astype(f32).astype(bf16)
    none = jnp.zeros_like(times)
    values = jnp.concatenate([t_all, s_all, to_t, to_s, first, none, none, none], axis=0)
    got = lax.dot_general(values.astype(bf16), mine, NT, preferred_element_type=f32)
    lanes = lax.broadcasted_iota(jnp.int32, (1, LIST), 1)
    nth = lanes.astype(f32) - 1.0 - got[4:5]
    t, s = got[0:1].astype(jnp.int32), got[1:2].astype(jnp.int32)
    taken = got[2:3] + got[3:4] > 0.0
    da = jnp.where(taken & (nth < got[2:3]), t, dump)
    db = jnp.where(taken & (nth < got[3:4]), s, dump)
    entries = t | s << 5 | da << 10 | db << 15
    count = jnp.sum(times, axis=1, keepdims=True).astype(jnp.int32)
    ahead = pairs + HALO * leaves
    chip = jnp.sum(times[:, :ahead], axis=1, keepdims=True).astype(jnp.int32)
    inner = jnp.sum(times[:, :pairs], axis=1, keepdims=True).astype(jnp.int32)
    for at, value in ((COUNT, count), (CHIP, chip), (INNER, inner), (SMALL, small)):
        entries = jnp.where(lanes == at, value, entries)
    return entries


def receive(on_chip, devices, dev, box, src, listed, v_all, rows, xyz, todo, wide, fetch):
    own = v_all.shape[0] - 2 * HALO
    size = v_all.shape[2]
    rhs = v_all.shape[1]
    half = HALO * size
    odd = dev[0] & 1
    side = 1 - odd if on_chip else odd
    edge = (dev[0] == 0) | (dev[0] == devices - 1)
    pts = src[rhs : rhs + 16, 0:half].astype(f32)
    coords, low, high = [], [], []
    centre = [box[6 + c : 7 + c, 0:1] for c in range(3)]
    for c in range(3):
        p = pts[c : c + 1] + pts[c + 3 : c + 4] + pts[c + 6 : c + 7]
        if not on_chip:
            p = jnp.where(edge, centre[c], p)
        low.append(jnp.minimum(box[c : c + 1, 0:1], jnp.min(p, axis=1, keepdims=True)))
        high.append(jnp.maximum(box[3 + c : 4 + c, 0:1], jnp.max(p, axis=1, keepdims=True)))
        coords.append(p)
    write_box(wide, low, high, centre)
    lane = lax.broadcasted_iota(jnp.int32, listed.shape, 1)
    todo[...] = jnp.where(lane == SMALL, is_small(low, high), listed[...])
    fetch.start()
    feat = row_features(*[p - c for p, c in zip(coords, centre)]).astype(bf16)
    full = jnp.concatenate([*coords, jnp.zeros((5, half), f32)], axis=0)
    for k in range(HALO):
        part = slice(k * size, (k + 1) * size)
        at = own + side * HALO + k
        v_all[at] = src[0:rhs, part]
        rows[at] = feat[:, part]
        xyz[at] = full[:, part]
    fetch.wait()


def near_piece(bounds, first, on_chip, devices, *refs):
    tile_q, tile_f, todo, sem = refs[-4:]
    if on_chip is None:
        listed, cols, rows, v_all, xyz = refs[:5]
        acc = refs[-5]
        fetch = pltpu.make_async_copy(listed, todo, sem)
        fetch.start()
        if first:
            acc[...] = jnp.zeros_like(acc)
        fetch.wait()
    else:
        dev, box, src, listed, cols = refs[:5]
        v_all, rows, xyz, acc, listed_out, wide = refs[-10:-4]
        fetch = pltpu.make_async_copy(listed_out, todo, sem)
        receive(on_chip, devices, dev, box, src, listed, v_all, rows, xyz, listed_out, wide, fetch)
    small = todo[0, SMALL] != 0
    n = todo[0, COUNT]
    steps = (n + UNROLL - 1) // UNROLL
    lo, hi = bounds(todo[0, INNER] // UNROLL, todo[0, CHIP] // UNROLL, steps)
    size = cols.shape[1]

    def entry(i):
        return todo[0, i + 1]

    def distances(code, slot):
        tile_q[slot] = jnp.dot(
            cols[code & 31], rows[(code >> 5) & 31], preferred_element_type=f32
        )

    def kernel_values(slot):
        for r in range(0, size, 64):
            part = tile_q[slot, r : r + 64]
            s = part + SHIFT
            y = s * s
            p = (y + B2) * y + s
            tile_f[slot, r : r + 64] = (((p + 2.0 * B0) * p + LAST) * lax.rsqrt(part)).astype(bf16)

    def apply(code, slot):
        t, s = code & 31, (code >> 5) & 31
        to_t, to_s = (code >> 10) & 31, (code >> 15) & 31
        acc[to_t] += lax.dot_general(v_all[s], tile_f[slot], NT, preferred_element_type=f32)
        acc[to_s] += jnp.dot(v_all[t], tile_f[slot], preferred_element_type=f32)

    @pl.when(small & (hi > lo))
    def _():
        tile_f[1] = jnp.zeros_like(tile_f[1])
        distances(entry(lo * UNROLL), 0)

        def step(i, _):
            base = i * UNROLL
            for j in range(UNROLL):
                a, b = j % 2, 1 - j % 2
                distances(entry(base + j + 1), b)
                kernel_values(a)
                apply(entry(base + j - 1), b)
            return 0

        lax.fori_loop(lo, hi, step, 0)
        apply(entry(hi * UNROLL - 1), (UNROLL - 1) % 2)

    @pl.when(jnp.logical_not(small))
    def _():
        def step(i, _):
            code = entry(i)
            t, s = code & 31, (code >> 5) & 31
            here, there = xyz[t], xyz[s]
            squared = jnp.zeros((size, size), f32)
            for c in range(3):
                along = jnp.transpose(jnp.broadcast_to(here[c : c + 1], (size, size)))
                spread = along - there[c : c + 1]
                squared = squared + spread * spread
            tile_q[0] = squared
            for r in range(0, size, 8):
                part = tile_q[0, r : r + 8]
                tile_q[1, r : r + 8] = (
                    jnp.cos(WAVE * jnp.sqrt(part)) * lax.rsqrt(part + CORE2) * SCALE
                )
            tile_f[0] = tile_q[1].astype(bf16)
            apply(code, 0)
            return 0

        lax.fori_loop(lo * UNROLL, jnp.minimum(hi * UNROLL, n), step, 0)


def mm(a, b):
    return jnp.dot(a, b, preferred_element_type=f32)


def lift(pair, even, odd):
    out = lax.dot_general(pair[0], even, TN, preferred_element_type=f32)
    out = out + lax.dot_general(pair[1], odd, TN, preferred_element_type=f32)
    return out.astype(bf16)


def first_step(dev, upper, moment, chip, out):
    rank, rhs = moment.shape
    half = chip.shape[1] - 128
    odd = (dev[0] & 1) == 1
    m0, other = moment[...], chip[0:rank, half : half + rhs]
    pair = (jnp.where(odd, other, m0), jnp.where(odd, m0, other))
    out[0], out[1] = pair
    out[2] = lift((upper[0, 0, 0], upper[0, 0, 1]), *pair)


def next_step(step, dev, upper, own, got, out):
    k = 2 * step
    low = ((dev[0] >> step) & 1) == 0
    pair = (jnp.where(low, own[k], got[k]), jnp.where(low, got[k], own[k]))
    out[0:k] = own[0:k]
    out[k], out[k + 1] = pair
    if out.shape[0] > k + 2:
        out[k + 2] = lift((upper[step, 0, 0], upper[step, 0, 1]), *pair)


def finish(levels, has_upper, refs):
    dev, upper, coupling, transfer, basis, acc = refs[:6]
    gots = refs[6:-3]
    out, held, sems = refs[-3:]
    d = dev[0]
    terms = []
    for b in range(levels):
        zero = jnp.zeros(gots[0].shape[1:], bf16)
        left, right = [zero, zero], [zero, zero]
        for step in range(b + 1, len(gots) + 1):
            got, k = gots[step - 1], 2 * b
            low = ((d >> step) & 1) == 0
            full = (1 << (step - 1 - b)) - 1
            inner = (d >> (b + 1)) & full
            before = jnp.logical_not(low) & (inner == 0)
            after = low & (inner == full)
            for i in range(2):
                left[i] = jnp.where(before, got[k + i], left[i])
                right[i] = jnp.where(after, got[k + i], right[i])
        crossed = jnp.where(((d >> b) & 1) == 1, left[1], right[0])
        terms.append(
            mm(coupling[b, 0, 0], left[0])
            + mm(coupling[b, 0, 1], crossed)
            + mm(coupling[b, 0, 2], right[1])
        )
    coeffs = terms[levels - 1]
    for b in range(has_upper - 1, -1, -1):
        coeffs = terms[b] + mm(upper[b, 0, (d >> b) & 1], coeffs.astype(bf16))
    words = coeffs.astype(bf16)
    leaves, rank, _ = transfer.shape
    leaf_coef = mm(transfer[...].reshape(leaves * rank, -1), words).astype(bf16)
    size = acc.shape[2]
    copies = []
    for t in range(leaves):
        part = slice(t * size, (t + 1) * size)
        far = lax.dot_general(
            leaf_coef[t * rank : (t + 1) * rank], basis[:, part], TN, preferred_element_type=f32
        )
        held[:, part] = (acc[t] + far).astype(bf16)
        if (t + 1) % 4 == 0:
            done = pl.ds((t - 3) * size, 4 * size)
            copies.append(pltpu.make_async_copy(held.at[:, done], out.at[:, done], sems.at[t // 4]))
            copies[-1].start()
    for copy in copies:
        copy.wait()


def on_device(devices, nodes, inputs, basis, transfer, upper, coupling, near_cols, near_count):
    leaves, rank, _ = transfer.shape
    rhs = inputs.shape[0]
    size = nodes.shape[1] // leaves
    half = HALO * size
    levels, ups = coupling.shape[0], upper.shape[0]
    dev = lax.axis_index("leaf").astype(jnp.int32).reshape(1)
    S = jax.ShapeDtypeStruct

    to_chip, to_next, v_all, xyz, box, moment = call(
        prepare, "prepare",
        (S((rhs + 16, half + 128), bf16), S((rhs + 16, half), bf16), S((leaves + 2 * HALO, rhs, size), bf16),
         S((leaves + 2 * HALO, 8, size), f32), S((16, 128), f32), S((rank, rhs), bf16)),
        [SM] + [HBM] * 4, (VM,) * 6,
        [pltpu.VMEM(nodes.shape, f32), pltpu.VMEM(inputs.shape, bf16), pltpu.VMEM(basis.shape, bf16),
         pltpu.VMEM(transfer.shape, bf16), pltpu.SemaphoreType.DMA((4,))], us=2,
    )(dev, *map(in_hbm, (nodes, inputs, basis, transfer)))
    chip = lax.ppermute(to_chip, "leaf", [(i, i ^ 1) for i in range(devices)])
    acc_shape = S((leaves + 1, rhs, size), f32)

    scratch = [
        pltpu.VMEM((2, size, size), f32), pltpu.VMEM((2, size, size), bf16),
        pltpu.SMEM((1, LIST), jnp.int32), pltpu.SemaphoreType.DMA,
    ]

    def near(name, bounds, us, acc=None):
        more = () if acc is None else (acc,)
        return call(
            functools.partial(near_piece, bounds, acc is None, None, devices), name, acc_shape,
            [VM] * (5 + len(more)), VM, scratch, {5: 0} if more else None, us=us,
        )(todo, cols, rows, v_all, xyz, *more)

    def near_after(name, bounds, us, on_chip, sent, acc):
        halo = (v_all, rows, xyz, acc)
        return call(
            functools.partial(near_piece, bounds, False, on_chip, devices), name,
            (*[S(a.shape, a.dtype) for a in halo], S(todo.shape, jnp.int32), S(box.shape, f32)),
            [SM] + [VM] * 8, (VM,) * 6, scratch, {5: 0, 6: 1, 7: 2, 8: 3}, us=us,
        )(dev, box, sent, todo, cols, *halo)

    def upto(k):
        return lambda inner, chip: jnp.minimum(jnp.minimum(FIRST, inner) + k * NEXT, chip)

    pieces_of = [
        lambda inner, chip, steps: (upto(0)(inner, chip), upto(1)(inner, chip)),
        lambda inner, chip, steps: (upto(1)(inner, chip), upto(2)(inner, chip)),
        lambda inner, chip, steps: (upto(2)(inner, chip), chip),
        lambda inner, chip, steps: (chip, steps),
    ]
    rows, cols, todo, acc = call(
        arrange, "arrange",
        (S((leaves + 2 * HALO, KF, size), bf16), S((leaves, size, KF), bf16), S((1, LIST), jnp.int32), acc_shape),
        [SM] + [VM] * 4, (VM,) * 4, us=2,
    )(dev, xyz, box, near_cols, near_count.reshape(1, leaves))
    acc, chip, moment = lax.optimization_barrier((acc, chip, moment))

    def block_count(step):
        return 2 * step + (1 if step < levels else 0)

    own = call(
        first_step, "first_step", S((block_count(1), rank, rhs), bf16), [SM, VM, VM, VM], VM
    )(dev, upper, moment, chip)
    own, chip = lax.optimization_barrier((own, chip))
    gots = []
    for step in range(1, levels + 1):
        mirror = (2 << step) - 2
        got = lax.ppermute(own, "leaf", [(i, i ^ mirror) for i in range(devices)])
        if step == levels:
            acc, beside = lax.optimization_barrier((acc, beside))
        if step in (1, levels):
            sent = chip if step == 1 else beside
            v_all, rows, xyz, acc, todo, box = near_after(f"near_{step}", pieces_of[min(step, 4) - 1], 4, step == 1, sent, acc)
        elif step < 4:
            acc = near(f"near_{step}", pieces_of[step - 1], 3, acc)
        if step == BESIDE:
            to_next, acc = lax.optimization_barrier((to_next, acc))
            beside = lax.ppermute(
                to_next, "leaf",
                [p for i in range(1, devices - 1, 2) for p in ((i, i + 1), (i + 1, i))],
            )
        own, got, acc = lax.optimization_barrier((own, got, acc))
        if step < levels:
            own = call(
                functools.partial(next_step, step), "next_step",
                S((block_count(step + 1), rank, rhs), bf16), [SM, VM, VM, VM], VM,
            )(dev, upper, own, got)
            own, acc = lax.optimization_barrier((own, acc))
        gots.append(got)

    return call(
        lambda *refs: finish(levels, ups, refs), "finish", S((rhs, leaves * size), bf16),
        [SM] + [VM] * (5 + len(gots)), HBM,
        [pltpu.VMEM((rhs, leaves * size), bf16), pltpu.SemaphoreType.DMA((leaves // 4,))], us=2,
    )(dev, upper, coupling, transfer, basis, acc, *gots)


def solution(mesh):
    placed = (
        P(None, "leaf"),
        P(None, "leaf"),
        P(None, "leaf"),
        P("leaf", None, None),
        P(None, "leaf", None, None, None),
        P(None, "leaf", None, None, None),
        P("leaf", None),
        P("leaf"),
    )
    return jax.shard_map(
        functools.partial(on_device, mesh.shape["leaf"]),
        mesh=mesh, in_specs=placed, out_specs=P(None, "leaf"), check_vma=False,
    )
```
